32 devices in a mesh: tgt: 16 (over z, y, core), sup: 2 (over x).
Axes of the slice: x: 2, y: 2, z: 4, core: 2. Of those that a mesh axis runs over, the one named last changes fastest.
Arguments:
- targets: float32 [128, 3, 1024], P('tgt'), may hold values from -4 to 4
- labels: int32 [128], P('tgt'), may hold values from 0 to 99
- support_slots: float32 [16, 64, 3, 1024], P('tgt', 'sup'), may hold values from -4 to 4
- block_owner: int32 [4], replicated, may hold values from 0 to 15, as said below
- dual_coeffs: float32 [4, 64, 100], P(None, 'sup'), may hold values from -0.15 to 0.15
Outputs:
- predictions: float32 [128, 100], P('tgt')
- support_grad: float32 [4, 64, 3, 1024], P(None, 'sup')
The draws below stay inside these ranges and needn't reach their ends.
Inputs may be any that keep to these rules, and one draw needn't show every extreme that they name: 4 distinct slot indices, among them 0 and 15; block b is support_slots[block_owner[b]], and the other slots are never read.
All inputs are finite; a program needn't handle non-finite values.
Results may differ from the reference program's by a relative error of at most 0.0001.
Values sent between devices are 32-bit elements; how exact they have to be, the bound alone decides.
A program may use at most 128 MiB of HBM per device.

```python
import jax
import jax.numpy as jnp
from jax import lax

SIDE = 32
CH = 3
CLASSES = 100
LAYERS = 3
BLOCKS = 4
SB = 64
TGT_DEV = 8
PIX = 1024
TARGETS = 128
N_TGT = 16


def draw_block_owner(key, part):
    middle = jax.random.permutation(jax.random.fold_in(key, 17), N_TGT - 2)[:BLOCKS - 2] + 1
    ends = jnp.array([0, N_TGT - 1], dtype=jnp.int32)
    values = jnp.concatenate([ends, middle.astype(jnp.int32)])
    order = jax.random.permutation(jax.random.fold_in(key, 23), BLOCKS)
    return values[order].astype(jnp.int32)


def set_ends(values, key, least, high):
    place = [jax.random.randint(jax.random.fold_in(key, axis), (), 0, length) for axis, length in enumerate(values.shape)]
    longest = values.shape.index(max(values.shape))
    neighbour = place[:longest] + [(place[longest] + 1) % values.shape[longest]] + place[longest + 1:]
    return values.at[tuple(place)].set(least).at[tuple(neighbour)].set(high)


def block_levels(own_key, shape, split, smallest, high):
    def one(dim, parts):
        heights = jax.random.uniform(jax.random.fold_in(jax.random.fold_in(own_key, 6), dim), (parts,), jnp.float32, smallest / len(split), high / len(split))
        return jnp.repeat(jnp.exp(heights), shape[dim] // parts).reshape((-1,) + (1,) * (len(shape) - dim - 1))

    gain = one(*split[0])
    for cut in split[1:]:
        gain = gain * one(*cut)
    return gain


def noise(rng, shape, spread, reach, shards=(), kind=jnp.bfloat16):
    loudness = block_levels(rng, shape, shards, -0.22, 0.18) if shards else 1.0
    entries = jax.random.normal(rng, shape, jnp.float32) * spread * loudness
    return jnp.minimum(jnp.maximum(entries, -reach), reach).astype(kind)


def setup_inputs(seed: int = 0) -> dict:
    streams_of = jax.random.split(jax.random.key(seed), 6)
    return {
        "targets": noise(streams_of[0], (TARGETS, CH, PIX), 1.0, 4.0, ((0, 16),), jnp.float32),
        "labels": set_ends(jax.random.randint(streams_of[1], (TARGETS,), 0, CLASSES), jax.random.fold_in(streams_of[1], 1), 0, CLASSES - 1).astype(jnp.int32),
        "support_slots": noise(streams_of[2], (N_TGT, SB, CH, PIX), 1.0, 4.0, ((0, 16), (1, 2)), jnp.float32),
        "block_owner": draw_block_owner(jax.random.fold_in(streams_of[5], 71), 0),
        "dual_coeffs": noise(streams_of[4], (BLOCKS, SB, CLASSES), 0.03, 0.15, ((1, 2),), jnp.float32),
    }


weight_variance = 1.6
bias_variance = 0.1
loss_weight = 64.0
arcsin_scale = 2.0 / 3.141592653589793

def box_sum(states, grid_side):
    length = states.shape[-1]
    column = lax.broadcasted_iota(jnp.int32, (length,), 0) % grid_side
    zero_column = jnp.zeros(states.shape[:-1] + (1,), states.dtype)
    from_left = jnp.where(column > 0, jnp.concatenate([zero_column, states[..., :-1]], axis=-1), 0.0)
    from_right = jnp.where(column < grid_side - 1, jnp.concatenate([states[..., 1:], zero_column], axis=-1), 0.0)
    row_sum = states + from_left + from_right
    zero_row = jnp.zeros(states.shape[:-1] + (grid_side,), states.dtype)
    from_above = jnp.concatenate([zero_row, row_sum[..., :-grid_side]], axis=-1)
    from_below = jnp.concatenate([row_sum[..., grid_side:], zero_row], axis=-1)
    return row_sum + from_above + from_below

def self_chain(images):
    squares = images[:, 0, :] * images[:, 0, :]
    for channel in range(1, images.shape[1]):
        squares = squares + images[:, channel, :] * images[:, channel, :]
    variance = weight_variance * box_sum(squares / images.shape[1], SIDE) / 9.0 + bias_variance
    variances = [variance]
    for layer_index in range(1, LAYERS):
        activated = arcsin_scale * jnp.arcsin(2.0 * variance / (1.0 + 2.0 * variance))
        variance = weight_variance * box_sum(activated, SIDE) / 9.0 + bias_variance
        variances.append(variance)
    return variances

def pair_kernel(support, support_variances, targets, target_variances):
    cross_terms = targets[:, 0, :][:, None, :] * support[:, 0, :][None, :, :]
    for channel in range(1, support.shape[1]):
        cross_terms = cross_terms + targets[:, channel, :][:, None, :] * support[:, channel, :][None, :, :]
    preact = weight_variance * box_sum(cross_terms / support.shape[1], SIDE) / 9.0 + bias_variance
    tangent = preact
    activated = preact
    slope = preact
    for layer_index in range(LAYERS):
        product = (1.0 + 2.0 * target_variances[layer_index])[:, None, :] * (1.0 + 2.0 * support_variances[layer_index])[None, :, :]
        activated = arcsin_scale * jnp.arcsin(2.0 * preact / jnp.sqrt(product))
        slope = 2.0 * arcsin_scale / jnp.sqrt(product - 4.0 * preact * preact)
        if layer_index + 1 < LAYERS:
            preact_next = weight_variance * box_sum(activated, SIDE) / 9.0 + bias_variance
            tangent = preact_next + weight_variance * box_sum(tangent * slope, SIDE) / 9.0
            preact = preact_next
    return lax.optimization_barrier(jnp.mean(weight_variance * (activated + tangent * slope) + bias_variance, axis=-1))

def reference(targets, labels, support_slots, block_owner, dual_coeffs):
    support = support_slots[block_owner].reshape(BLOCKS * SB, CH, PIX)
    coeffs = dual_coeffs.reshape(BLOCKS * SB, CLASSES)
    support_variances, self_pullback = jax.vjp(self_chain, support)
    target_groups = targets.reshape(N_TGT, TGT_DEV, CH, PIX)

    def forward_group(carry, target_group):
        target_variances = self_chain(target_group)
        return (carry, pair_kernel(support, support_variances, target_group, target_variances))
    unused, kernel_rows = lax.scan(forward_group, jnp.zeros((), jnp.float32), target_groups)
    kernel_all = kernel_rows.reshape(TARGETS, BLOCKS * SB)
    predictions = jnp.dot(kernel_all, coeffs, precision=lax.Precision.HIGHEST)
    onehot = (labels[:, None] == lax.broadcasted_iota(jnp.int32, (1, CLASSES), 1)).astype(jnp.float32)
    residual_error = loss_weight * (predictions - onehot)
    pair_weights = jnp.dot(residual_error, coeffs.T, precision=lax.Precision.HIGHEST).reshape(N_TGT, TGT_DEV, BLOCKS * SB)

    def backward_group(carry, inputs):
        target_group, weights = inputs
        target_variances = self_chain(target_group)

        def kernel_rows_of(images, variances):
            return pair_kernel(images, variances, target_group, target_variances)
        unused_kernel, pullback = jax.vjp(kernel_rows_of, support, support_variances)
        grad_images, grad_variances = pullback(weights)
        summed = [total_part + grad_part for total_part, grad_part in zip(carry[1], grad_variances)]
        return ((carry[0] + grad_images, summed), None)
    initial = (jnp.zeros_like(support), [jnp.zeros_like(variance) for variance in support_variances])
    totals, unused_rows = lax.scan(backward_group, initial, (target_groups, pair_weights))
    gradient = totals[0] + self_pullback(totals[1])[0]
    return (predictions, gradient.reshape(BLOCKS, SB, CH, PIX))
```

```python
import functools

import jax
import jax.numpy as jnp
from jax import lax
from jax.experimental import pallas as pl
from jax.experimental.pallas import tpu as pltpu
from jax.sharding import PartitionSpec as P

SIDE = 32
LANES = 128
CHUNK = 8
MESH = pl.DeviceIdType.MESH

weight_variance = 1.6
bias_variance = 0.1
loss_weight = 64.0
q = 2.0 / 3.141592653589793
w9 = weight_variance / 9.0

HALF = (
    0.9999998807907104, 0.16668881475925446, 0.07438822090625763,
    0.05069158226251602, 0.0044584982098147, 0.06837297230958939,
)
MIDDLE = (
    1.0000003576278687, 0.16661593317985535, 0.0763598307967186, 0.03124197944998741,
    0.09119893610477448, -0.11032058298587799, 0.1385442167520523,
)
LAST = (
    0.9999997615814209, 0.16670268774032593, 0.07408007979393005,
    0.0530407689511776, -0.0027404483407735825, 0.07600238919258118,
)


def polynomial(x, coefficients):
    total = jnp.full_like(x, coefficients[-1])
    for value in coefficients[-2::-1]:
        total = total * x + value
    return total


def wide_arcsin(z, complement, r):
    cosine = complement * r
    half = z * lax.rsqrt(2.0 + 2.0 * cosine)
    return (half + half) * polynomial(0.5 - 0.5 * cosine, HALF)


def target_factors(targets):
    def box(x):
        image = x.reshape(-1, SIDE, SIDE)
        padded = jnp.pad(image, ((0, 0), (1, 1), (1, 1)))
        rows = padded[:, :-2] + padded[:, 1:-1] + padded[:, 2:]
        return (rows[:, :, :-2] + rows[:, :, 1:-1] + rows[:, :, 2:]).reshape(x.shape)

    n = w9 * box(jnp.sum(targets * targets, axis=1) / targets.shape[1]) + bias_variance
    factors = [lax.rsqrt(1.0 + 2.0 * n)]
    for _ in range(2):
        n = w9 * box(q * jnp.arcsin(2.0 * n / (1.0 + 2.0 * n))) + bias_variance
        factors.append(lax.rsqrt(1.0 + 2.0 * n))
    return factors


def all_reduce_body(sizes, x_ref, out_ref, *scratch):
    stages = len(sizes)
    received = scratch[:stages]
    partial = scratch[stages:2 * stages - 1]
    send_sem, recv_sem, send_back, recv_back = scratch[2 * stages - 1:]
    me = lax.axis_index("tgt")
    digits, strides = [], []
    stride = 1
    for size in sizes:
        digits.append(lax.rem(me // stride, size))
        strides.append(stride)
        stride = stride * size

    def peer(stage, step):
        digit = lax.rem(digits[stage] + step, sizes[stage])
        return digit, me + (digit - digits[stage]) * strides[stage]

    barrier = pltpu.get_barrier_semaphore()
    greeted = 0
    for stage, size in enumerate(sizes):
        for step in range(1, size):
            pl.semaphore_signal(
                barrier, inc=1, device_id={"tgt": peer(stage, step)[1]}, device_id_type=MESH
            )
            greeted += 1
    pl.semaphore_wait(barrier, greeted)

    rows = x_ref.shape[0]
    held = x_ref
    base = 0
    index = 0
    bases = []
    for stage, size in enumerate(sizes):
        rows = rows // size
        copies = []
        for step in range(1, size):
            digit, device = peer(stage, step)
            copy = pltpu.make_async_remote_copy(
                src_ref=held.at[pl.ds(pl.multiple_of(digit * rows, 8), rows)],
                dst_ref=received[stage].at[size - 1 - step],
                send_sem=send_sem.at[index],
                recv_sem=recv_sem.at[index + size - 2 * step],
                device_id={"tgt": device},
                device_id_type=MESH,
            )
            copy.start()
            copies.append(copy)
            index += 1
        total = held[pl.ds(pl.multiple_of(digits[stage] * rows, 8), rows)]
        for copy in copies:
            copy.wait()
        for slot in range(size - 1):
            total = total + received[stage][slot]
        bases.append(base)
        base = base + digits[stage] * rows
        if stage + 1 < stages:
            partial[stage][...] = total
            held = partial[stage]
        else:
            out_ref[pl.ds(pl.multiple_of(base, 8), rows)] = total
    index = 0
    for stage in reversed(range(stages)):
        size = sizes[stage]
        place = pl.ds(pl.multiple_of(bases[stage] + digits[stage] * rows, 8), rows)
        copies = []
        for step in range(1, size):
            copy = pltpu.make_async_remote_copy(
                src_ref=out_ref.at[place],
                dst_ref=out_ref.at[place],
                send_sem=send_back.at[index],
                recv_sem=recv_back.at[index],
                device_id={"tgt": peer(stage, step)[1]},
                device_id_type=MESH,
            )
            copy.start()
            copies.append(copy)
            index += 1
        for copy in copies:
            copy.wait()
        rows = rows * size


def all_reduce(x, devices, collective_id):
    bits = devices.bit_length() - 1
    low = max((bits - 1) // 2, 0)
    sizes = [size for size in (min(devices, 2), 2 ** low, 2 ** (bits - 1 - low)) if size > 1]
    rows = x.shape[0]
    received, partial = [], []
    for size in sizes:
        rows = rows // size
        received.append(pltpu.VMEM((size - 1, rows, LANES), jnp.float32))
        partial.append(pltpu.VMEM((rows, LANES), jnp.float32))
    copies = sum(size - 1 for size in sizes)
    return pl.pallas_call(
        functools.partial(all_reduce_body, sizes),
        out_shape=jax.ShapeDtypeStruct(x.shape, x.dtype),
        in_specs=[pl.BlockSpec(memory_space=pltpu.VMEM)],
        out_specs=pl.BlockSpec(memory_space=pltpu.VMEM),
        scratch_shapes=received + partial[:-1] + [pltpu.SemaphoreType.DMA((copies,))] * 4,
        compiler_params=pltpu.CompilerParams(
            collective_id=collective_id, has_side_effects=True, vmem_limit_bytes=24 << 20
        ),
        name="sum_over_targets",
    )(x)


def tangent_body(
    n_sup, channels, s_ref, t_ref, u_ref, label_ref, coeff_ref, pred_ref, grad_ref,
    f1, f2, f3, f4, z1_ref, z2_ref, th2_ref, n3_ref, sb_ref, vb_ref, sf_ref, nb_ref, part_ref,
    arrived, send_sem, recv_sem,
):
    pixels = SIDE * SIDE
    me = lax.axis_index("sup")
    barrier = pltpu.get_barrier_semaphore()
    for step in range(1, n_sup):
        pl.semaphore_signal(
            barrier, inc=1, device_id={"sup": lax.rem(me + step, n_sup)}, device_id_type=MESH
        )

    for field in (f1, f2, f3, f4):
        for row in (0, SIDE + 1):
            field[row] = jnp.zeros(field.shape[1:], jnp.float32)

        def border(row, carry, field=field):
            for column in (0, SIDE + 1):
                field[row, column] = jnp.zeros(field.shape[2:], jnp.float32)
            return carry

        lax.fori_loop(1, SIDE + 1, border, 0)

    zero_row = jnp.zeros((SIDE, LANES), jnp.float32)
    for slot in range(2):
        sf_ref[slot, pl.ds(0, SIDE)] = zero_row
        sf_ref[slot, pl.ds(SIDE + pixels, SIDE)] = zero_row
    column = lax.broadcasted_iota(jnp.int32, (SIDE, LANES), 0)

    def line(row):
        return pl.ds(pl.multiple_of(row * SIDE, SIDE), SIDE)

    def flat_box(slot, row):
        x = (
            sf_ref[slot, line(row)] + sf_ref[slot, line(row + 1)] + sf_ref[slot, line(row + 2)]
        )
        left = jnp.where(column == 0, 0.0, pltpu.roll(x, 1, 0))
        right = jnp.where(column == SIDE - 1, 0.0, pltpu.roll(x, SIDE - 1, 0))
        return x + left + right

    def squares(row, carry):
        total = jnp.zeros((SIDE, LANES), jnp.float32)
        for c in range(channels):
            image = s_ref[c, line(row)]
            total = total + image * image
            for j in range(SIDE):
                sb_ref[c, row * SIDE + j] = image[j:j + 1]
        sf_ref[0, line(row + 1)] = total
        return carry

    lax.fori_loop(0, SIDE, squares, 0)

    def own_layer(layer):
        source, target = layer % 2, (layer + 1) % 2
        scale = w9 / channels if layer == 0 else w9 * q

        def body(row, carry):
            n = scale * flat_box(source, row) + bias_variance
            b = 1.0 + 2.0 * n
            v = lax.rsqrt(b)
            nb_ref[layer, line(row)] = n
            for j in range(SIDE):
                vb_ref[layer, row * SIDE + j] = v[j:j + 1]
            if layer < 2:
                z = 2.0 * n / b
                if layer == 0:
                    complement = 1.0 - z * z
                    angle = wide_arcsin(z, complement, lax.rsqrt(complement))
                else:
                    angle = z * polynomial(z * z, MIDDLE)
                sf_ref[target, line(row + 1)] = angle
            return carry

        lax.fori_loop(0, SIDE, body, 0)

    for layer in range(3):
        own_layer(layer)

    def rows(function, init=0):
        return lax.fori_loop(0, SIDE, function, init)

    def spread(ref, k, row, c0):
        values = ref[k, row]
        return jnp.stack(
            [jnp.broadcast_to(values[:, c0 + j:c0 + j + 1], (8, LANES)) for j in range(CHUNK)]
        )

    def across(ref, k, row, c0):
        values = ref[k, pl.ds(row * SIDE + c0, CHUNK)]
        return jnp.broadcast_to(values, (CHUNK, 8, LANES))

    def box(ref, row, c0):
        x = (
            ref[row, pl.ds(c0, CHUNK + 2)]
            + ref[row + 1, pl.ds(c0, CHUNK + 2)]
            + ref[row + 2, pl.ds(c0, CHUNK + 2)]
        )
        return x[:-2] + x[1:-1] + x[2:]

    def put(ref, row, c0, value):
        ref[row + 1, pl.ds(c0 + 1, CHUNK)] = value

    starts = range(0, SIDE, CHUNK)

    def pass_cross(row, carry):
        for c0 in starts:
            total = spread(t_ref, 0, row, c0) * across(sb_ref, 0, row, c0)
            for c in range(1, channels):
                total = total + spread(t_ref, c, row, c0) * across(sb_ref, c, row, c0)
            put(f1, row, c0, total)
        return carry

    def pass_first(row, carry):
        for c0 in starts:
            uv = spread(u_ref, 0, row, c0) * across(vb_ref, 0, row, c0)
            z = uv * ((2.0 * w9 / channels) * box(f1, row, c0) + 2.0 * bias_variance)
            complement = 1.0 - z * z
            r = lax.rsqrt(complement)
            z1_ref[row, pl.ds(c0, CHUNK)] = z
            put(f2, row, c0, wide_arcsin(z, complement, r))
            put(f3, row, c0, z * r)
        return carry

    def pass_second(row, carry):
        for c0 in starts:
            uv = spread(u_ref, 1, row, c0) * across(vb_ref, 1, row, c0)
            z = uv * ((2.0 * w9 * q) * box(f2, row, c0) + 2.0 * bias_variance)
            tangent = z + uv * ((2.0 * w9 * q) * box(f3, row, c0))
            square = z * z
            r = lax.rsqrt(1.0 - square)
            z2_ref[row, pl.ds(c0, CHUNK)] = z
            th2_ref[row, pl.ds(c0, CHUNK)] = tangent
            put(f1, row, c0, z * polynomial(square, MIDDLE))
            put(f4, row, c0, tangent * r)
        return carry

    def pass_third(row, carry):
        for c0 in starts:
            uv = spread(u_ref, 2, row, c0) * across(vb_ref, 2, row, c0)
            z = uv * ((2.0 * w9 * q) * box(f1, row, c0) + 2.0 * bias_variance)
            tangent = z + uv * ((2.0 * w9 * q) * box(f4, row, c0))
            square = z * z
            r = lax.rsqrt(1.0 - square)
            carry = carry + jnp.sum(z * polynomial(square, LAST) + tangent * r, axis=0)
            slope = (2.0 * q * w9) * (uv * r)
            bent = tangent * (r * r)
            put(f3, row, c0, slope)
            put(f2, row, c0, slope * (2.0 + z * bent))
            n3_ref[row, pl.ds(c0, CHUNK)] = r * (z + bent)
        return carry

    rows(pass_cross)
    rows(pass_first)
    rows(pass_second)
    mean = rows(pass_third, jnp.zeros((8, LANES), jnp.float32))
    kernel = (weight_variance * q / pixels) * mean + bias_variance

    part_ref[...] = jnp.dot(
        kernel, coeff_ref[...], precision=lax.Precision.HIGHEST,
        preferred_element_type=jnp.float32,
    )
    pl.semaphore_wait(barrier, n_sup - 1)
    copies = []
    for step in range(1, n_sup):
        copy = pltpu.make_async_remote_copy(
            src_ref=part_ref,
            dst_ref=arrived.at[step - 1],
            send_sem=send_sem.at[step - 1],
            recv_sem=recv_sem.at[step - 1],
            device_id={"sup": lax.rem(me + step, n_sup)},
            device_id_type=MESH,
        )
        copy.start()
        copies.append(copy)
    for copy in copies:
        copy.wait()
    predictions = part_ref[...]
    for step in range(n_sup - 1):
        predictions = predictions + arrived[step]
    pred_ref[...] = predictions
    onehot = (label_ref[...] == lax.broadcasted_iota(jnp.int32, (8, LANES), 1)).astype(jnp.float32)
    error = loss_weight * (predictions - onehot)
    weights = lax.dot_general(
        error, coeff_ref[...], (((1,), (1,)), ((), ())), precision=lax.Precision.HIGHEST,
        preferred_element_type=jnp.float32,
    )
    kappa = (weight_variance / pixels) * weights

    def total_rows(value):
        return jnp.sum(value, axis=1)

    def pass_back_second(row, carry):
        for c0 in starts:
            uv = spread(u_ref, 1, row, c0) * across(vb_ref, 1, row, c0)
            z = z2_ref[row, pl.ds(c0, CHUNK)]
            tangent = th2_ref[row, pl.ds(c0, CHUNK)]
            r = lax.rsqrt(1.0 - z * z)
            up = kappa * box(f2, row, c0)
            mean_up = kappa * box(f3, row, c0)
            bent = mean_up * tangent * (r * r)
            slope = (2.0 * q * w9) * (uv * r)
            put(f4, row, c0, mean_up * slope)
            put(f1, row, c0, slope * (up + mean_up + bent * z))
            place = pl.ds(pl.multiple_of(row * SIDE + c0, CHUNK), CHUNK)
            nb_ref[4, place] = total_rows(r * (up * z + bent))
            nb_ref[5, place] = total_rows(kappa * n3_ref[row, pl.ds(c0, CHUNK)])
        return carry

    def pass_back_first(row, carry):
        for c0 in starts:
            uv = spread(u_ref, 0, row, c0) * across(vb_ref, 0, row, c0)
            z = z1_ref[row, pl.ds(c0, CHUNK)]
            r = lax.rsqrt(1.0 - z * z)
            joined = r * (box(f1, row, c0) + (r * r) * box(f4, row, c0))
            put(f2, row, c0, (2.0 * q * w9 / channels) * (uv * joined))
            place = pl.ds(pl.multiple_of(row * SIDE + c0, CHUNK), CHUNK)
            nb_ref[3, place] = total_rows(z * joined)
        return carry

    rows(pass_back_second)
    rows(pass_back_first)

    def own_back(layer):
        source, target = (layer + 1) % 2, layer % 2

        def body(row, carry):
            n = nb_ref[layer, line(row)]
            b = 1.0 + 2.0 * n
            value = nb_ref[3 + layer, line(row)] * (-q / b)
            if layer < 2:
                value = value + (2.0 * w9 * q) * flat_box(source, row) * (
                    lax.rsqrt(1.0 + 4.0 * n) / b
                )
            sf_ref[target, line(row + 1)] = value
            return carry

        lax.fori_loop(0, SIDE, body, 0)

    for layer in (2, 1, 0):
        own_back(layer)

    def pass_images(row, carry):
        own = (2.0 * w9 / channels) * flat_box(0, row)
        for c in range(channels):
            grad_ref[c, line(row)] = own * s_ref[c, line(row)]
        for c0 in starts:
            value = box(f2, row, c0)
            place = pl.ds(pl.multiple_of(row * SIDE + c0, CHUNK), CHUNK)
            for c in range(channels):
                grad_ref[c, place] += total_rows(value * spread(t_ref, c, row, c0))
        return carry

    rows(pass_images)


def tangent(s, t, u, labels, coeffs, n_sup):
    channels = s.shape[0]
    pixels = SIDE * SIDE
    field = pltpu.VMEM((SIDE + 2, SIDE + 2, 8, LANES), jnp.float32)
    plain = pltpu.VMEM((SIDE, SIDE, 8, LANES), jnp.float32)
    vmem = pl.BlockSpec(memory_space=pltpu.VMEM)
    return pl.pallas_call(
        functools.partial(tangent_body, n_sup, channels),
        out_shape=(
            jax.ShapeDtypeStruct((8, LANES), jnp.float32),
            jax.ShapeDtypeStruct((channels, pixels, LANES), jnp.float32),
        ),
        in_specs=[vmem] * 5,
        out_specs=(vmem, vmem),
        scratch_shapes=[field] * 4 + [plain] * 4 + [
            pltpu.VMEM((channels, pixels, 1, LANES), jnp.float32),
            pltpu.VMEM((3, pixels, 1, LANES), jnp.float32),
            pltpu.VMEM((2, pixels + 2 * SIDE, LANES), jnp.float32),
            pltpu.VMEM((6, pixels, LANES), jnp.float32),
            pltpu.VMEM((8, LANES), jnp.float32),
            pltpu.VMEM((n_sup - 1, 8, LANES), jnp.float32),
            pltpu.SemaphoreType.DMA((n_sup - 1,)),
            pltpu.SemaphoreType.DMA((n_sup - 1,)),
        ],
        compiler_params=pltpu.CompilerParams(
            collective_id=1, has_side_effects=True, vmem_limit_bytes=60 << 20
        ),
        name="tangent_kernel",
    )(s, t, u, labels, coeffs)


def local(n_tgt, n_sup, targets, labels, support_slots, block_owner, dual_coeffs):
    blocks, per_block, classes = dual_coeffs.shape
    channels = targets.shape[1]
    pixels = targets.shape[2]
    supports = blocks * per_block
    mine = block_owner == lax.axis_index("tgt")
    slot = jnp.transpose(support_slots[0], (1, 2, 0))
    own = jnp.where(mine[None, None, :, None], slot[:, :, None, :], 0.0)
    own = own.reshape(channels * pixels, supports)
    own = jnp.pad(own, ((0, 0), (0, LANES - supports)))
    s = all_reduce(own, n_tgt, 0).reshape(channels, pixels, LANES)

    def by_row(x):
        return jnp.transpose(x.reshape(x.shape[0], SIDE, SIDE), (1, 0, 2))

    t = jnp.stack([by_row(targets[:, c]) for c in range(channels)])
    u = jnp.stack([by_row(x) for x in target_factors(targets)])
    coeffs = jnp.pad(
        dual_coeffs.reshape(supports, classes), ((0, LANES - supports), (0, LANES - classes))
    )
    predictions, grad = tangent(s, t, u, labels[:, None], coeffs, n_sup)
    grad = all_reduce(grad.reshape(channels * pixels, LANES), n_tgt, 2)
    grad = grad[:, :supports].reshape(channels, pixels, blocks, per_block)
    return predictions[:, :classes], jnp.transpose(grad, (2, 3, 0, 1))


def solution(mesh):
    return jax.shard_map(
        functools.partial(local, mesh.shape["tgt"], mesh.shape["sup"]),
        mesh=mesh,
        in_specs=(
            P("tgt", None, None),
            P("tgt"),
            P("tgt", "sup", None, None),
            P(),
            P(None, "sup", None),
        ),
        out_specs=(P("tgt", None), P(None, "sup", None, None)),
        check_vma=False,
    )
```

```python
import functools

import jax
import jax.numpy as jnp
from jax import lax
from jax.experimental import pallas as pl
from jax.experimental.pallas import tpu as pltpu
from jax.sharding import PartitionSpec as P

SIDE = 32
LANES = 128
CHUNK = 8
MESH = pl.DeviceIdType.MESH

weight_variance = 1.6
bias_variance = 0.1
loss_weight = 64.0
q = 2.0 / 3.141592653589793
w9 = weight_variance / 9.0

HALF = (
    0.9999998807907104, 0.16668881475925446, 0.07438822090625763,
    0.05069158226251602, 0.0044584982098147, 0.06837297230958939,
)
MIDDLE = (
    1.0000003576278687, 0.16661593317985535, 0.0763598307967186, 0.03124197944998741,
    0.09119893610477448, -0.11032058298587799, 0.1385442167520523,
)
LAST = (
    0.9999997615814209, 0.16670268774032593, 0.07408007979393005,
    0.0530407689511776, -0.0027404483407735825, 0.07600238919258118,
)


def polynomial(x, coefficients):
    total = jnp.full_like(x, coefficients[-1])
    for value in coefficients[-2::-1]:
        total = total * x + value
    return total


def wide_arcsin(z, complement, r):
    cosine = complement * r
    half = z * lax.rsqrt(2.0 + 2.0 * cosine)
    return (half + half) * polynomial(0.5 - 0.5 * cosine, HALF)


def target_factors(targets):
    def box(x):
        image = x.reshape(-1, SIDE, SIDE)
        padded = jnp.pad(image, ((0, 0), (1, 1), (1, 1)))
        rows = padded[:, :-2] + padded[:, 1:-1] + padded[:, 2:]
        return (rows[:, :, :-2] + rows[:, :, 1:-1] + rows[:, :, 2:]).reshape(x.shape)

    n = w9 * box(jnp.sum(targets * targets, axis=1) / targets.shape[1]) + bias_variance
    factors = [lax.rsqrt(1.0 + 2.0 * n)]
    for _ in range(2):
        n = w9 * box(q * jnp.arcsin(2.0 * n / (1.0 + 2.0 * n))) + bias_variance
        factors.append(lax.rsqrt(1.0 + 2.0 * n))
    return factors


def stage_sizes(devices):
    bits = devices.bit_length() - 1
    low = max((bits - 1) // 2, 0)
    return [size for size in (min(devices, 2), 2 ** low, 2 ** (bits - 1 - low)) if size > 1]


class Stages:
    def __init__(self, sizes):
        self.sizes = sizes
        self.me = lax.axis_index("tgt")
        self.strides, self.digits = [], []
        stride = 1
        for size in sizes:
            self.strides.append(stride)
            self.digits.append(lax.rem(self.me // stride, size))
            stride = stride * size

    def place(self, device):
        total = 0
        for size, stride in zip(self.sizes, self.strides):
            total = total * size + lax.rem(device // stride, size)
        return total

    def peer(self, stage, step):
        digit = lax.rem(self.digits[stage] + step, self.sizes[stage])
        return digit, self.me + (digit - self.digits[stage]) * self.strides[stage]

    def base(self, stage, rows):
        total = 0
        for size, digit in zip(self.sizes[:stage + 1], self.digits):
            rows = rows // size
            total = total + digit * rows
        return total

    def back_copies(self, out_ref, piece, first, rows, stage, send, receive):
        held = rows
        for size in self.sizes[:stage + 1]:
            held = held // size
        place = pl.ds(pl.multiple_of(first + self.base(stage, rows), 8), held)
        before = sum(size - 1 for size in self.sizes[:stage])
        copies = []
        for step in range(1, self.sizes[stage]):
            copies.append(pltpu.make_async_remote_copy(
                src_ref=out_ref.at[place],
                dst_ref=out_ref.at[place],
                send_sem=send.at[piece, before + step - 1],
                recv_sem=receive.at[piece, before + step - 1],
                device_id={"tgt": self.peer(stage, step)[1]},
                device_id_type=MESH,
            ))
        return copies


def start_all(copies):
    for copy in copies:
        copy.start()
    return copies


def all_reduce_body(sizes, pieces, x_ref, out_ref, *scratch):
    stages = len(sizes)
    received = scratch[:stages]
    partial = scratch[stages:2 * stages - 1]
    send_sem, recv_sem, send_back, recv_back = scratch[2 * stages - 1:]
    where = Stages(sizes)
    barrier = pltpu.get_barrier_semaphore()
    for stage, size in enumerate(sizes):
        for step in range(1, size):
            pl.semaphore_signal(
                barrier, inc=1, device_id={"tgt": where.peer(stage, step)[1]},
                device_id_type=MESH,
            )
    pl.semaphore_wait(barrier, sum(size - 1 for size in sizes))
    rows = x_ref.shape[0] // pieces
    held = [rows]
    for size in sizes:
        held.append(held[-1] // size)

    def source(stage, piece):
        if stage == 0:
            return x_ref.at[pl.ds(piece * rows, rows)]
        return partial[stage - 1].at[piece]

    def send(stage, piece):
        size = sizes[stage]
        before = sum(other - 1 for other in sizes[:stage])
        copies = []
        for step in range(1, size):
            digit, device = where.peer(stage, step)
            part = pl.ds(pl.multiple_of(digit * held[stage + 1], 8), held[stage + 1])
            copies.append(pltpu.make_async_remote_copy(
                src_ref=source(stage, piece).at[part],
                dst_ref=received[stage].at[piece, step - 1],
                send_sem=send_sem.at[piece, before + step - 1],
                recv_sem=recv_sem.at[piece, before + step - 1],
                device_id={"tgt": device},
                device_id_type=MESH,
            ))
        return start_all(copies)

    def add(stage, piece, copies):
        part = pl.ds(
            pl.multiple_of(where.digits[stage] * held[stage + 1], 8), held[stage + 1]
        )
        total = source(stage, piece)[part]
        for copy in copies:
            copy.wait()
        for slot in range(sizes[stage] - 1):
            total = total + received[stage][piece, slot]
        if stage + 1 < stages:
            partial[stage][piece] = total
        else:
            place = pl.multiple_of(piece * rows + where.base(stage, rows), 8)
            out_ref[pl.ds(place, held[stage + 1])] = total

    def back(step, piece):
        return start_all(where.back_copies(
            out_ref, piece, piece * rows, rows, stages - 1 - step, send_back, recv_back
        ))

    pending = [send(0, piece) for piece in range(pieces)]
    for tick in range(pieces + 2 * stages - 1):
        for piece in range(pieces):
            level = tick - piece
            if level < 0 or level >= 2 * stages:
                continue
            if level < stages:
                add(level, piece, pending[piece])
            else:
                for copy in pending[piece]:
                    copy.wait()
            if level + 1 < stages:
                pending[piece] = send(level + 1, piece)
            elif level + 1 < 2 * stages:
                pending[piece] = back(level + 1 - stages, piece)


def all_reduce(x, devices, collective_id, pieces=3):
    sizes = stage_sizes(devices)
    rows = x.shape[0] // pieces
    received, partial = [], []
    for size in sizes:
        rows = rows // size
        received.append(pltpu.VMEM((pieces, size - 1, rows, LANES), jnp.float32))
        partial.append(pltpu.VMEM((pieces, rows, LANES), jnp.float32))
    copies = sum(size - 1 for size in sizes)
    return pl.pallas_call(
        functools.partial(all_reduce_body, sizes, pieces),
        out_shape=jax.ShapeDtypeStruct(x.shape, x.dtype),
        in_specs=[pl.BlockSpec(memory_space=pltpu.VMEM)],
        out_specs=pl.BlockSpec(memory_space=pltpu.VMEM),
        scratch_shapes=received + partial[:-1] + [pltpu.SemaphoreType.DMA((pieces, copies))] * 4,
        compiler_params=pltpu.CompilerParams(
            collective_id=collective_id, has_side_effects=True, vmem_limit_bytes=24 << 20
        ),
        name="sum_over_targets",
    )(x)


def gather_body(devices, channels, blocks, owner_ref, x_ref, out_ref, slots, *semaphores):
    send_sem, recv_sem, send_back, recv_back = semaphores
    sizes = stage_sizes(devices)
    stages = len(sizes)
    where = Stages(sizes)
    me = where.me
    barrier = pltpu.get_barrier_semaphore()
    for step in range(1, devices):
        pl.semaphore_signal(
            barrier, inc=1, device_id={"tgt": lax.rem(me + step, devices)}, device_id_type=MESH
        )
    pl.semaphore_wait(barrier, devices - 1)
    copies = []
    for step in range(1, devices):
        device = lax.rem(me + step, devices)
        copies.append(pltpu.make_async_remote_copy(
            src_ref=x_ref.at[where.place(device)],
            dst_ref=slots.at[me],
            send_sem=send_sem.at[step - 1],
            recv_sem=recv_sem.at[step - 1],
            device_id={"tgt": device},
            device_id_type=MESH,
        ))
    start_all(copies)
    slots[me] = x_ref[where.place(me)]
    for copy in copies:
        copy.wait()
    rows = out_ref.shape[0] // channels
    chunk = rows // devices
    packed = x_ref.shape[1] // channels
    groups = chunk // packed
    width = LANES // groups
    block = lax.broadcasted_iota(jnp.int32, (packed, LANES), 1) // width
    base = where.base(stages - 1, rows)
    pending = []
    for c in range(channels):
        parts = [slots[owner_ref[b], pl.ds(c * packed, packed)] for b in range(blocks)]
        for k in range(groups):
            total = jnp.zeros((packed, LANES), jnp.float32)
            for b in range(blocks):
                shift = (width * (b - k)) % LANES
                moved = pltpu.roll(parts[b], shift, 1) if shift else parts[b]
                total = jnp.where(block == b, moved, total)
            out_ref[pl.ds(pl.multiple_of(c * rows + base + k * packed, 8), packed)] = total
        pending.append(start_all(where.back_copies(
            out_ref, c, c * rows, rows, stages - 1, send_back, recv_back
        )))
    for tick in range(channels + stages - 1):
        for c in range(channels):
            level = tick - c
            if level < 0 or level >= stages:
                continue
            for copy in pending[c]:
                copy.wait()
            if level + 1 < stages:
                pending[c] = start_all(where.back_copies(
                    out_ref, c, c * rows, rows, stages - 2 - level, send_back, recv_back
                ))


def gather(slot, owner, devices):
    per_block, channels, pixels = slot.shape
    blocks = owner.shape[0]
    groups = LANES // per_block
    packed = pixels // devices // groups
    x = slot.reshape(per_block, channels, devices, groups, packed)
    x = jnp.transpose(x, (2, 1, 4, 3, 0)).reshape(devices, channels * packed, LANES)
    copies = sum(size - 1 for size in stage_sizes(devices))
    vmem = pl.BlockSpec(memory_space=pltpu.VMEM)
    return pl.pallas_call(
        functools.partial(gather_body, devices, channels, blocks),
        out_shape=jax.ShapeDtypeStruct((channels * pixels, LANES), jnp.float32),
        in_specs=[pl.BlockSpec(memory_space=pltpu.SMEM), vmem],
        out_specs=vmem,
        scratch_shapes=[
            pltpu.VMEM(x.shape, jnp.float32),
            pltpu.SemaphoreType.DMA((devices - 1,)),
            pltpu.SemaphoreType.DMA((devices - 1,)),
            pltpu.SemaphoreType.DMA((channels, copies)),
            pltpu.SemaphoreType.DMA((channels, copies)),
        ],
        compiler_params=pltpu.CompilerParams(
            collective_id=0, has_side_effects=True, vmem_limit_bytes=24 << 20
        ),
        name="gather_supports",
    )(owner, x)


def tangent_body(
    n_sup, channels, s_ref, t_ref, u_ref, label_ref, coeff_ref, pred_ref, grad_ref,
    f1, f2, f3, f4, z1_ref, z2_ref, th2_ref, n3_ref, sb_ref, vb_ref, sf_ref, nb_ref, sum_ref, part_ref,
    arrived, send_sem, recv_sem,
):
    pixels = SIDE * SIDE
    me = lax.axis_index("sup")
    barrier = pltpu.get_barrier_semaphore()
    for step in range(1, n_sup):
        pl.semaphore_signal(
            barrier, inc=1, device_id={"sup": lax.rem(me + step, n_sup)}, device_id_type=MESH
        )

    for field in (f1, f2, f3, f4):
        for row in (0, SIDE + 1):
            field[row] = jnp.zeros(field.shape[1:], jnp.float32)

        def border(row, carry, field=field):
            for column in (0, SIDE + 1):
                field[row, column] = jnp.zeros(field.shape[2:], jnp.float32)
            return carry

        lax.fori_loop(1, SIDE + 1, border, 0)

    zero_row = jnp.zeros((SIDE, LANES), jnp.float32)
    for slot in range(2):
        sf_ref[slot, pl.ds(0, SIDE)] = zero_row
        sf_ref[slot, pl.ds(SIDE + pixels, SIDE)] = zero_row
    column = lax.broadcasted_iota(jnp.int32, (SIDE, LANES), 0)

    def line(row):
        return pl.ds(pl.multiple_of(row * SIDE, SIDE), SIDE)

    def flat_box(slot, row):
        x = (
            sf_ref[slot, line(row)] + sf_ref[slot, line(row + 1)] + sf_ref[slot, line(row + 2)]
        )
        left = jnp.where(column == 0, 0.0, pltpu.roll(x, 1, 0))
        right = jnp.where(column == SIDE - 1, 0.0, pltpu.roll(x, SIDE - 1, 0))
        return x + left + right

    def squares(row, carry):
        total = jnp.zeros((SIDE, LANES), jnp.float32)
        for c in range(channels):
            image = s_ref[c, line(row)]
            total = total + image * image
            for j in range(SIDE):
                sb_ref[c, row * SIDE + j] = image[j:j + 1]
        sf_ref[0, line(row + 1)] = total
        return carry

    lax.fori_loop(0, SIDE, squares, 0)

    def own_layer(layer):
        source, target = layer % 2, (layer + 1) % 2
        scale = w9 / channels if layer == 0 else w9 * q

        def body(row, carry):
            n = scale * flat_box(source, row) + bias_variance
            b = 1.0 + 2.0 * n
            v = lax.rsqrt(b)
            nb_ref[layer, line(row)] = n
            for j in range(SIDE):
                vb_ref[layer, row * SIDE + j] = v[j:j + 1]
            if layer < 2:
                z = 2.0 * n / b
                if layer == 0:
                    complement = 1.0 - z * z
                    angle = wide_arcsin(z, complement, lax.rsqrt(complement))
                else:
                    angle = z * polynomial(z * z, MIDDLE)
                sf_ref[target, line(row + 1)] = angle
            return carry

        lax.fori_loop(0, SIDE, body, 0)

    for layer in range(3):
        own_layer(layer)

    def rows(function, init=0):
        return lax.fori_loop(0, SIDE, function, init)

    def spread(ref, k, row, c0):
        values = ref[k, row]
        return jnp.stack(
            [jnp.broadcast_to(values[:, c0 + j:c0 + j + 1], (8, LANES)) for j in range(CHUNK)]
        )

    def across(ref, k, row, c0):
        values = ref[k, pl.ds(row * SIDE + c0, CHUNK)]
        return jnp.broadcast_to(values, (CHUNK, 8, LANES))

    def box(ref, row, c0):
        x = (
            ref[row, pl.ds(c0, CHUNK + 2)]
            + ref[row + 1, pl.ds(c0, CHUNK + 2)]
            + ref[row + 2, pl.ds(c0, CHUNK + 2)]
        )
        return x[:-2] + x[1:-1] + x[2:]

    def put(ref, row, c0, value):
        ref[row + 1, pl.ds(c0 + 1, CHUNK)] = value

    starts = range(0, SIDE, CHUNK)

    def pass_cross(row, carry):
        for c0 in starts:
            total = spread(t_ref, 0, row, c0) * across(sb_ref, 0, row, c0)
            for c in range(1, channels):
                total = total + spread(t_ref, c, row, c0) * across(sb_ref, c, row, c0)
            put(f1, row, c0, total)
        return carry

    def pass_first(row, carry):
        for c0 in starts:
            uv = spread(u_ref, 0, row, c0) * across(vb_ref, 0, row, c0)
            z = uv * ((2.0 * w9 / channels) * box(f1, row, c0) + 2.0 * bias_variance)
            complement = 1.0 - z * z
            r = lax.rsqrt(complement)
            z1_ref[row, pl.ds(c0, CHUNK)] = z
            put(f2, row, c0, wide_arcsin(z, complement, r))
            put(f3, row, c0, z * r)
        return carry

    def pass_second(row, carry):
        for c0 in starts:
            uv = spread(u_ref, 1, row, c0) * across(vb_ref, 1, row, c0)
            z = uv * ((2.0 * w9 * q) * box(f2, row, c0) + 2.0 * bias_variance)
            tangent = z + uv * ((2.0 * w9 * q) * box(f3, row, c0))
            square = z * z
            r = lax.rsqrt(1.0 - square)
            z2_ref[row, pl.ds(c0, CHUNK)] = z
            th2_ref[row, pl.ds(c0, CHUNK)] = tangent
            put(f1, row, c0, z * polynomial(square, MIDDLE))
            put(f4, row, c0, tangent * r)
        return carry

    def pass_third(row, carry):
        for c0 in starts:
            uv = spread(u_ref, 2, row, c0) * across(vb_ref, 2, row, c0)
            z = uv * ((2.0 * w9 * q) * box(f1, row, c0) + 2.0 * bias_variance)
            tangent = z + uv * ((2.0 * w9 * q) * box(f4, row, c0))
            square = z * z
            r = lax.rsqrt(1.0 - square)
            carry = carry + jnp.sum(z * polynomial(square, LAST) + tangent * r, axis=0)
            slope = (2.0 * q * w9) * (uv * r)
            bent = tangent * (r * r)
            put(f3, row, c0, slope)
            put(f2, row, c0, slope * (2.0 + z * bent))
            n3_ref[row, pl.ds(c0, CHUNK)] = r * (z + bent)
        return carry

    rows(pass_cross)
    rows(pass_first)
    rows(pass_second)
    mean = rows(pass_third, jnp.zeros((8, LANES), jnp.float32))
    kernel = (weight_variance * q / pixels) * mean + bias_variance

    part_ref[...] = jnp.dot(
        kernel, coeff_ref[...], precision=lax.Precision.HIGHEST,
        preferred_element_type=jnp.float32,
    )
    pl.semaphore_wait(barrier, n_sup - 1)
    copies = []
    for step in range(1, n_sup):
        copy = pltpu.make_async_remote_copy(
            src_ref=part_ref,
            dst_ref=arrived.at[step - 1],
            send_sem=send_sem.at[step - 1],
            recv_sem=recv_sem.at[step - 1],
            device_id={"sup": lax.rem(me + step, n_sup)},
            device_id_type=MESH,
        )
        copy.start()
        copies.append(copy)
    for copy in copies:
        copy.wait()
    predictions = part_ref[...]
    for step in range(n_sup - 1):
        predictions = predictions + arrived[step]
    pred_ref[...] = predictions
    onehot = (label_ref[...] == lax.broadcasted_iota(jnp.int32, (8, LANES), 1)).astype(jnp.float32)
    error = loss_weight * (predictions - onehot)
    weights = lax.dot_general(
        error, coeff_ref[...], (((1,), (1,)), ((), ())), precision=lax.Precision.HIGHEST,
        preferred_element_type=jnp.float32,
    )
    kappa = (weight_variance / pixels) * weights

    sublane = lax.broadcasted_iota(jnp.int32, (8, LANES), 0)
    odd = [lax.rem(sublane // step, 2) == 1 for step in (1, 2, 4)]

    def total_rows(value):
        items = [value[j] for j in range(CHUNK)]
        for step, mask in zip((1, 2, 4), odd):
            items = [
                jnp.where(mask, second, first)
                + pltpu.roll(jnp.where(mask, first, second), step, 0)
                for first, second in zip(items[::2], items[1::2])
            ]
        return items[0]

    def pass_back_second(row, carry):
        for c0 in starts:
            uv = spread(u_ref, 1, row, c0) * across(vb_ref, 1, row, c0)
            z = z2_ref[row, pl.ds(c0, CHUNK)]
            tangent = th2_ref[row, pl.ds(c0, CHUNK)]
            r = lax.rsqrt(1.0 - z * z)
            up = kappa * box(f2, row, c0)
            mean_up = kappa * box(f3, row, c0)
            bent = mean_up * tangent * (r * r)
            slope = (2.0 * q * w9) * (uv * r)
            put(f4, row, c0, mean_up * slope)
            put(f1, row, c0, slope * (up + mean_up + bent * z))
            place = pl.ds(pl.multiple_of(row * SIDE + c0, CHUNK), CHUNK)
            nb_ref[4, place] = total_rows(r * (up * z + bent))
            nb_ref[5, place] = total_rows(kappa * n3_ref[row, pl.ds(c0, CHUNK)])
        return carry

    def pass_back_first(row, carry):
        for c0 in starts:
            uv = spread(u_ref, 0, row, c0) * across(vb_ref, 0, row, c0)
            z = z1_ref[row, pl.ds(c0, CHUNK)]
            r = lax.rsqrt(1.0 - z * z)
            joined = r * (box(f1, row, c0) + (r * r) * box(f4, row, c0))
            put(f2, row, c0, (2.0 * q * w9 / channels) * (uv * joined))
            place = pl.ds(pl.multiple_of(row * SIDE + c0, CHUNK), CHUNK)
            nb_ref[3, place] = total_rows(z * joined)
        return carry

    rows(pass_back_second)
    rows(pass_back_first)

    def own_back(layer):
        source, target = (layer + 1) % 2, layer % 2

        def body(row, carry):
            n = nb_ref[layer, line(row)]
            b = 1.0 + 2.0 * n
            value = nb_ref[3 + layer, line(row)] * (-q / b)
            if layer < 2:
                value = value + (2.0 * w9 * q) * flat_box(source, row) * (
                    lax.rsqrt(1.0 + 4.0 * n) / b
                )
            sf_ref[target, line(row + 1)] = value
            return carry

        lax.fori_loop(0, SIDE, body, 0)

    for layer in (2, 1, 0):
        own_back(layer)

    def pass_images(row, carry):
        own = (2.0 * w9 / channels) * flat_box(0, row)
        for c in range(channels):
            sum_ref[c, line(row)] = own * s_ref[c, line(row)]
        for c0 in starts:
            value = box(f2, row, c0)
            place = pl.ds(pl.multiple_of(row * SIDE + c0, CHUNK), CHUNK)
            for c in range(channels):
                sum_ref[c, place] += total_rows(value * spread(t_ref, c, row, c0))
        return carry

    rows(pass_images)
    for c in range(channels):
        def turn(group, carry, c=c):
            place = pl.ds(pl.multiple_of(group * LANES, LANES), LANES)
            grad_ref[c * (pixels // LANES) + group] = jnp.transpose(sum_ref[c, place])
            return carry

        lax.fori_loop(0, pixels // LANES, turn, 0)


def tangent(s, t, u, labels, coeffs, n_sup):
    channels = s.shape[0]
    pixels = SIDE * SIDE
    field = pltpu.VMEM((SIDE + 2, SIDE + 2, 8, LANES), jnp.float32)
    plain = pltpu.VMEM((SIDE, SIDE, 8, LANES), jnp.float32)
    vmem = pl.BlockSpec(memory_space=pltpu.VMEM)
    return pl.pallas_call(
        functools.partial(tangent_body, n_sup, channels),
        out_shape=(
            jax.ShapeDtypeStruct((8, LANES), jnp.float32),
            jax.ShapeDtypeStruct((channels * pixels // LANES, LANES, LANES), jnp.float32),
        ),
        in_specs=[vmem] * 5,
        out_specs=(vmem, vmem),
        scratch_shapes=[field] * 4 + [plain] * 4 + [
            pltpu.VMEM((channels, pixels, 1, LANES), jnp.float32),
            pltpu.VMEM((3, pixels, 1, LANES), jnp.float32),
            pltpu.VMEM((2, pixels + 2 * SIDE, LANES), jnp.float32),
            pltpu.VMEM((6, pixels, LANES), jnp.float32),
            pltpu.VMEM((channels, pixels, LANES), jnp.float32),
            pltpu.VMEM((8, LANES), jnp.float32),
            pltpu.VMEM((n_sup - 1, 8, LANES), jnp.float32),
            pltpu.SemaphoreType.DMA((n_sup - 1,)),
            pltpu.SemaphoreType.DMA((n_sup - 1,)),
        ],
        compiler_params=pltpu.CompilerParams(
            collective_id=1, has_side_effects=True, vmem_limit_bytes=60 << 20
        ),
        name="tangent_kernel",
    )(s, t, u, labels, coeffs)


def local(n_tgt, n_sup, targets, labels, support_slots, block_owner, dual_coeffs):
    blocks, per_block, classes = dual_coeffs.shape
    channels = targets.shape[1]
    pixels = targets.shape[2]
    supports = blocks * per_block
    if supports == LANES and (pixels * per_block) % (n_tgt * LANES * 8) == 0:
        s = gather(support_slots[0], block_owner, n_tgt)
    else:
        mine = block_owner == lax.axis_index("tgt")
        slot = jnp.transpose(support_slots[0], (1, 2, 0))
        own = jnp.where(mine[None, None, :, None], slot[:, :, None, :], 0.0)
        own = own.reshape(channels * pixels, supports)
        s = all_reduce(jnp.pad(own, ((0, 0), (0, LANES - supports))), n_tgt, 0)
    s = s.reshape(channels, pixels, LANES)

    def by_row(x):
        return jnp.transpose(x.reshape(x.shape[0], SIDE, SIDE), (1, 0, 2))

    t = jnp.stack([by_row(targets[:, c]) for c in range(channels)])
    u = jnp.stack([by_row(x) for x in target_factors(targets)])
    coeffs = jnp.pad(
        dual_coeffs.reshape(supports, classes), ((0, LANES - supports), (0, LANES - classes))
    )
    predictions, grad = tangent(s, t, u, labels[:, None], coeffs, n_sup)
    grad = all_reduce(grad.reshape(channels * pixels, LANES), n_tgt, 2)
    grad = grad.reshape(channels, pixels // LANES, LANES, LANES)[:, :, :supports]
    grad = jnp.transpose(grad, (2, 0, 1, 3)).reshape(blocks, per_block, channels, pixels)
    return predictions[:, :classes], grad


def solution(mesh):
    return jax.shard_map(
        functools.partial(local, mesh.shape["tgt"], mesh.shape["sup"]),
        mesh=mesh,
        in_specs=(
            P("tgt", None, None),
            P("tgt"),
            P("tgt", "sup", None, None),
            P(),
            P(None, "sup", None),
        ),
        out_specs=(P("tgt", None), P(None, "sup", None, None)),
        check_vma=False,
    )
```

```python
import functools

import jax
import jax.numpy as jnp
from jax import lax
from jax.experimental import pallas as pl
from jax.experimental.pallas import tpu as pltpu
from jax.sharding import PartitionSpec as P

SIDE = 32
LANES = 128
CHUNK = 8
MESH = pl.DeviceIdType.MESH

weight_variance = 1.6
bias_variance = 0.1
loss_weight = 64.0
q = 2.0 / 3.141592653589793
w9 = weight_variance / 9.0

HALF = (
    0.9999998807907104, 0.16668881475925446, 0.07438822090625763,
    0.05069158226251602, 0.0044584982098147, 0.06837297230958939,
)
MIDDLE = (
    1.0000003576278687, 0.16661593317985535, 0.0763598307967186, 0.03124197944998741,
    0.09119893610477448, -0.11032058298587799, 0.1385442167520523,
)
LAST = (
    0.9999997615814209, 0.16670268774032593, 0.07408007979393005,
    0.0530407689511776, -0.0027404483407735825, 0.07600238919258118,
)


def polynomial(x, coefficients):
    total = jnp.full_like(x, coefficients[-1])
    for value in coefficients[-2::-1]:
        total = total * x + value
    return total


def wide_arcsin(z, complement, r):
    cosine = complement * r
    half = z * lax.rsqrt(2.0 + 2.0 * cosine)
    return (half + half) * polynomial(0.5 - 0.5 * cosine, HALF)


def stage_sizes(devices):
    bits = devices.bit_length() - 1
    low = max((bits - 1) // 2, 0)
    return [size for size in (min(devices, 2), 2 ** low, 2 ** (bits - 1 - low)) if size > 1]


class Stages:
    def __init__(self, sizes):
        self.sizes = sizes
        self.me = lax.axis_index("tgt")
        self.strides, self.digits = [], []
        stride = 1
        for size in sizes:
            self.strides.append(stride)
            self.digits.append(lax.rem(self.me // stride, size))
            stride = stride * size

    def place(self, device):
        total = 0
        for size, stride in zip(self.sizes, self.strides):
            total = total * size + lax.rem(device // stride, size)
        return total

    def peer(self, stage, step):
        digit = lax.rem(self.digits[stage] + step, self.sizes[stage])
        return digit, self.me + (digit - self.digits[stage]) * self.strides[stage]

    def base(self, stage, rows):
        total = 0
        for size, digit in zip(self.sizes[:stage + 1], self.digits):
            rows = rows // size
            total = total + digit * rows
        return total

    def back_copies(self, out_ref, piece, first, rows, stage, send, receive):
        held = rows
        for size in self.sizes[:stage + 1]:
            held = held // size
        place = pl.ds(pl.multiple_of(first + self.base(stage, rows), 8), held)
        before = sum(size - 1 for size in self.sizes[:stage])
        copies = []
        for step in range(1, self.sizes[stage]):
            copies.append(pltpu.make_async_remote_copy(
                src_ref=out_ref.at[place],
                dst_ref=out_ref.at[place],
                send_sem=send.at[piece, before + step - 1],
                recv_sem=receive.at[piece, before + step - 1],
                device_id={"tgt": self.peer(stage, step)[1]},
                device_id_type=MESH,
            ))
        return copies


def start_all(copies):
    for copy in copies:
        copy.start()
    return copies


def all_reduce_body(sizes, pieces, x_ref, out_ref, *scratch):
    stages = len(sizes)
    received = scratch[:stages]
    partial = scratch[stages:2 * stages - 1]
    send_sem, recv_sem, send_back, recv_back = scratch[2 * stages - 1:]
    where = Stages(sizes)
    barrier = pltpu.get_barrier_semaphore()
    for stage, size in enumerate(sizes):
        for step in range(1, size):
            pl.semaphore_signal(
                barrier, inc=1, device_id={"tgt": where.peer(stage, step)[1]},
                device_id_type=MESH,
            )
    pl.semaphore_wait(barrier, sum(size - 1 for size in sizes))
    rows = x_ref.shape[0] // pieces
    held = [rows]
    for size in sizes:
        held.append(held[-1] // size)

    def source(stage, piece):
        if stage == 0:
            return x_ref.at[pl.ds(piece * rows, rows)]
        return partial[stage - 1].at[piece]

    def send(stage, piece):
        size = sizes[stage]
        before = sum(other - 1 for other in sizes[:stage])
        copies = []
        for step in range(1, size):
            digit, device = where.peer(stage, step)
            part = pl.ds(pl.multiple_of(digit * held[stage + 1], 8), held[stage + 1])
            copies.append(pltpu.make_async_remote_copy(
                src_ref=source(stage, piece).at[part],
                dst_ref=received[stage].at[piece, step - 1],
                send_sem=send_sem.at[piece, before + step - 1],
                recv_sem=recv_sem.at[piece, before + step - 1],
                device_id={"tgt": device},
                device_id_type=MESH,
            ))
        return start_all(copies)

    def add(stage, piece, copies):
        part = pl.ds(
            pl.multiple_of(where.digits[stage] * held[stage + 1], 8), held[stage + 1]
        )
        total = source(stage, piece)[part]
        for copy in copies:
            copy.wait()
        for slot in range(sizes[stage] - 1):
            total = total + received[stage][piece, slot]
        if stage + 1 < stages:
            partial[stage][piece] = total
        else:
            place = pl.multiple_of(piece * rows + where.base(stage, rows), 8)
            out_ref[pl.ds(place, held[stage + 1])] = total

    def back(step, piece):
        return start_all(where.back_copies(
            out_ref, piece, piece * rows, rows, stages - 1 - step, send_back, recv_back
        ))

    pending = [send(0, piece) for piece in range(pieces)]
    for tick in range(pieces + 2 * stages - 1):
        for piece in range(pieces):
            level = tick - piece
            if level < 0 or level >= 2 * stages:
                continue
            if level < stages:
                add(level, piece, pending[piece])
            else:
                for copy in pending[piece]:
                    copy.wait()
            if level + 1 < stages:
                pending[piece] = send(level + 1, piece)
            elif level + 1 < 2 * stages:
                pending[piece] = back(level + 1 - stages, piece)


def all_reduce(x, devices, collective_id):
    sizes = stage_sizes(devices)
    pieces = max(k for k in (1, 2, 3, 6) if x.shape[0] % (k * devices * 8) == 0)
    rows = x.shape[0] // pieces
    received, partial = [], []
    for size in sizes:
        rows = rows // size
        received.append(pltpu.VMEM((pieces, size - 1, rows, LANES), jnp.float32))
        partial.append(pltpu.VMEM((pieces, rows, LANES), jnp.float32))
    copies = sum(size - 1 for size in sizes)
    return pl.pallas_call(
        functools.partial(all_reduce_body, sizes, pieces),
        out_shape=jax.ShapeDtypeStruct(x.shape, x.dtype),
        in_specs=[pl.BlockSpec(memory_space=pltpu.VMEM)],
        out_specs=pl.BlockSpec(memory_space=pltpu.VMEM),
        scratch_shapes=received + partial[:-1] + [pltpu.SemaphoreType.DMA((pieces, copies))] * 4,
        compiler_params=pltpu.CompilerParams(
            collective_id=collective_id, has_side_effects=True, vmem_limit_bytes=24 << 20
        ),
        name="sum_over_targets",
    )(x)


def gather_body(devices, channels, blocks, owner_ref, x_ref, out_ref, *scratch):
    slots = scratch[:channels]
    send_sem, recv_sem, send_back, recv_back = scratch[channels:]
    sizes = stage_sizes(devices)
    stages = len(sizes)
    where = Stages(sizes)
    me = where.me
    barrier = pltpu.get_barrier_semaphore()
    for step in range(1, devices):
        pl.semaphore_signal(
            barrier, inc=1, device_id={"tgt": lax.rem(me + step, devices)}, device_id_type=MESH
        )
    pl.semaphore_wait(barrier, devices - 1)
    packed = x_ref.shape[1] // channels
    copies = []
    for c in range(channels):
        part = pl.ds(c * packed, packed)
        copies.append([])
        for step in range(1, devices):
            device = lax.rem(me + step, devices)
            copies[c].append(pltpu.make_async_remote_copy(
                src_ref=x_ref.at[where.place(device), part],
                dst_ref=slots[c].at[me],
                send_sem=send_sem.at[c, step - 1],
                recv_sem=recv_sem.at[c, step - 1],
                device_id={"tgt": device},
                device_id_type=MESH,
            ))
        start_all(copies[c])
    for c in range(channels):
        slots[c][me] = x_ref[where.place(me), pl.ds(c * packed, packed)]
    rows = out_ref.shape[0] // channels
    chunk = rows // devices
    groups = chunk // packed
    width = LANES // groups
    block = lax.broadcasted_iota(jnp.int32, (packed, LANES), 1) // width
    base = where.base(stages - 1, rows)
    pending = []
    for c in range(channels):
        for copy in copies[c]:
            copy.wait()
        parts = [slots[c][owner_ref[b]] for b in range(blocks)]
        for k in range(groups):
            total = jnp.zeros((packed, LANES), jnp.float32)
            for b in range(blocks):
                shift = (width * (b - k)) % LANES
                moved = pltpu.roll(parts[b], shift, 1) if shift else parts[b]
                total = jnp.where(block == b, moved, total)
            out_ref[pl.ds(pl.multiple_of(c * rows + base + k * packed, 8), packed)] = total
        pending.append(start_all(where.back_copies(
            out_ref, c, c * rows, rows, stages - 1, send_back, recv_back
        )))
    for tick in range(channels + stages - 1):
        for c in range(channels):
            level = tick - c
            if level < 0 or level >= stages:
                continue
            for copy in pending[c]:
                copy.wait()
            if level + 1 < stages:
                pending[c] = start_all(where.back_copies(
                    out_ref, c, c * rows, rows, stages - 2 - level, send_back, recv_back
                ))


def gather(slot, owner, devices):
    per_block, channels, pixels = slot.shape
    blocks = owner.shape[0]
    groups = LANES // per_block
    packed = pixels // devices // groups
    x = slot.reshape(per_block, channels, devices, groups, packed)
    x = jnp.transpose(x, (2, 1, 4, 3, 0)).reshape(devices, channels * packed, LANES)
    copies = sum(size - 1 for size in stage_sizes(devices))
    vmem = pl.BlockSpec(memory_space=pltpu.VMEM)
    return pl.pallas_call(
        functools.partial(gather_body, devices, channels, blocks),
        out_shape=jax.ShapeDtypeStruct((channels * pixels, LANES), jnp.float32),
        in_specs=[pl.BlockSpec(memory_space=pltpu.SMEM), vmem],
        out_specs=vmem,
        scratch_shapes=[pltpu.VMEM((devices, packed, LANES), jnp.float32)] * channels + [
            pltpu.SemaphoreType.DMA((channels, devices - 1)),
            pltpu.SemaphoreType.DMA((channels, devices - 1)),
            pltpu.SemaphoreType.DMA((channels, copies)),
            pltpu.SemaphoreType.DMA((channels, copies)),
        ],
        compiler_params=pltpu.CompilerParams(
            collective_id=0, has_side_effects=True, vmem_limit_bytes=24 << 20
        ),
        name="gather_supports",
    )(owner, x)


def tangent_body(
    n_sup, channels, s_ref, raw_ref, label_ref, dual_ref, pred_ref, grad_ref,
    f1, f2, f3, f4, z1_ref, r1_ref, z2_ref, r2_ref, th2_ref, n3_ref, t_ref, u_ref, sb_ref, vb_ref, sf_ref, nb_ref, sum_ref, part_ref,
    arrived, send_sem, recv_sem,
):
    pixels = SIDE * SIDE
    me = lax.axis_index("sup")
    barrier = pltpu.get_barrier_semaphore()
    for step in range(1, n_sup):
        pl.semaphore_signal(
            barrier, inc=1, device_id={"sup": lax.rem(me + step, n_sup)}, device_id_type=MESH
        )

    lane = lax.broadcasted_iota(jnp.int32, (8, LANES), 1)
    t_ref[...] = jnp.zeros(t_ref.shape, jnp.float32)
    for c in range(channels):
        image = raw_ref[:, c, :]
        for row in range(SIDE):
            t_ref[c, row, :, :SIDE] = image[:, row * SIDE:(row + 1) * SIDE]

    def lane_box(x):
        none = jnp.zeros((1, 8, LANES), jnp.float32)
        total = x + jnp.concatenate([none, x[:-1]]) + jnp.concatenate([x[1:], none])
        left = jnp.where(lane == 0, 0.0, pltpu.roll(total, 1, 2))
        right = jnp.where(lane == SIDE - 1, 0.0, pltpu.roll(total, LANES - 1, 2))
        return total + left + right

    power = t_ref[0] * t_ref[0]
    for c in range(1, channels):
        power = power + t_ref[c] * t_ref[c]
    n_t = (w9 / channels) * lane_box(power) + bias_variance
    for layer in range(3):
        b_t = 1.0 + 2.0 * n_t
        u_ref[layer] = lax.rsqrt(b_t)
        if layer < 2:
            z_t = 2.0 * n_t / b_t
            if layer == 0:
                rest = 1.0 - z_t * z_t
                angle_t = wide_arcsin(z_t, rest, lax.rsqrt(rest))
            else:
                angle_t = z_t * polynomial(z_t * z_t, MIDDLE)
            angle_t = jnp.where(lane < SIDE, angle_t, 0.0)
            n_t = (w9 * q) * lane_box(angle_t) + bias_variance

    for field in (f1, f2, f3, f4):
        for row in (0, SIDE + 1):
            field[row] = jnp.zeros(field.shape[1:], jnp.float32)

        def border(row, carry, field=field):
            for column in (0, SIDE + 1):
                field[row, column] = jnp.zeros(field.shape[2:], jnp.float32)
            return carry

        lax.fori_loop(1, SIDE + 1, border, 0)

    zero_row = jnp.zeros((SIDE, LANES), jnp.float32)
    for slot in range(2):
        sf_ref[slot, pl.ds(0, SIDE)] = zero_row
        sf_ref[slot, pl.ds(SIDE + pixels, SIDE)] = zero_row
    column = lax.broadcasted_iota(jnp.int32, (SIDE, LANES), 0)

    def line(row):
        return pl.ds(pl.multiple_of(row * SIDE, SIDE), SIDE)

    def flat_box(slot, row):
        x = (
            sf_ref[slot, line(row)] + sf_ref[slot, line(row + 1)] + sf_ref[slot, line(row + 2)]
        )
        left = jnp.where(column == 0, 0.0, pltpu.roll(x, 1, 0))
        right = jnp.where(column == SIDE - 1, 0.0, pltpu.roll(x, SIDE - 1, 0))
        return x + left + right

    def squares(row, carry):
        total = jnp.zeros((SIDE, LANES), jnp.float32)
        for c in range(channels):
            image = s_ref[c, line(row)]
            total = total + image * image
            for j in range(SIDE):
                sb_ref[c, row * SIDE + j] = image[j:j + 1]
        sf_ref[0, line(row + 1)] = total
        return carry

    lax.fori_loop(0, SIDE, squares, 0)

    def own_layer(layer):
        source, target = layer % 2, (layer + 1) % 2
        scale = w9 / channels if layer == 0 else w9 * q

        def body(row, carry):
            n = scale * flat_box(source, row) + bias_variance
            b = 1.0 + 2.0 * n
            v = lax.rsqrt(b)
            nb_ref[layer, line(row)] = n
            for j in range(SIDE):
                vb_ref[layer, row * SIDE + j] = v[j:j + 1]
            if layer < 2:
                z = 2.0 * n / b
                if layer == 0:
                    complement = 1.0 - z * z
                    angle = wide_arcsin(z, complement, lax.rsqrt(complement))
                else:
                    angle = z * polynomial(z * z, MIDDLE)
                sf_ref[target, line(row + 1)] = angle
            return carry

        lax.fori_loop(0, SIDE, body, 0)

    for layer in range(3):
        own_layer(layer)

    coeffs = dual_ref[...].reshape(-1, dual_ref.shape[2])
    if coeffs.shape[0] < LANES:
        coeffs = jnp.pad(coeffs, ((0, LANES - coeffs.shape[0]), (0, 0)))

    def rows(function, init=0):
        def two(step, carry):
            return function(step * 2, carry)

        return lax.fori_loop(0, SIDE // 2, two, init)

    def spread(ref, k, row, c0):
        values = ref[k, row]
        return jnp.stack(
            [jnp.broadcast_to(values[:, c0 + j:c0 + j + 1], (8, LANES)) for j in range(CHUNK)]
        )

    def across(ref, k, row, c0):
        values = ref[k, pl.ds(row * SIDE + c0, CHUNK)]
        return jnp.broadcast_to(values, (CHUNK, 8, LANES))

    def box(ref, row, c0):
        lines = [ref[row + k, pl.ds(c0, CHUNK + 2)] for k in range(4)]
        middle = lines[1] + lines[2]
        sums = [lines[0] + middle, middle + lines[3]]
        return [x[:-2] + x[1:-1] + x[2:] for x in sums]

    def put(ref, row, c0, value):
        ref[row + 1, pl.ds(c0 + 1, CHUNK)] = value

    def keep(ref, row, c0, value):
        ref[row, pl.ds(c0, CHUNK)] = value

    def kept(ref, row, c0):
        return ref[row, pl.ds(c0, CHUNK)]

    starts = range(0, SIDE, CHUNK)

    def pass_cross(first, carry):
        for row in (first, first + 1):
            for c0 in starts:
                total = spread(t_ref, 0, row, c0) * across(sb_ref, 0, row, c0)
                for c in range(1, channels):
                    total = total + spread(t_ref, c, row, c0) * across(sb_ref, c, row, c0)
                put(f1, row, c0, total)
        return carry

    def pass_first(first, carry):
        for c0 in starts:
            for row, value in zip((first, first + 1), box(f1, first, c0)):
                uv = spread(u_ref, 0, row, c0) * across(vb_ref, 0, row, c0)
                z = uv * ((2.0 * w9 / channels) * value + 2.0 * bias_variance)
                complement = 1.0 - z * z
                r = lax.rsqrt(complement)
                keep(z1_ref, row, c0, z)
                keep(r1_ref, row, c0, r)
                put(f2, row, c0, wide_arcsin(z, complement, r))
                put(f3, row, c0, z * r)
        return carry

    def pass_second(first, carry):
        for c0 in starts:
            pairs = zip((first, first + 1), box(f2, first, c0), box(f3, first, c0))
            for row, angles, tangents in pairs:
                uv = spread(u_ref, 1, row, c0) * across(vb_ref, 1, row, c0)
                z = uv * ((2.0 * w9 * q) * angles + 2.0 * bias_variance)
                tangent = z + uv * ((2.0 * w9 * q) * tangents)
                square = z * z
                r = lax.rsqrt(1.0 - square)
                keep(z2_ref, row, c0, z)
                keep(r2_ref, row, c0, r)
                keep(th2_ref, row, c0, tangent)
                put(f1, row, c0, z * polynomial(square, MIDDLE))
                put(f4, row, c0, tangent * r)
        return carry

    def pass_third(first, carry):
        for c0 in starts:
            pairs = zip((first, first + 1), box(f1, first, c0), box(f4, first, c0))
            for row, angles, tangents in pairs:
                uv = spread(u_ref, 2, row, c0) * across(vb_ref, 2, row, c0)
                z = uv * ((2.0 * w9 * q) * angles + 2.0 * bias_variance)
                tangent = z + uv * ((2.0 * w9 * q) * tangents)
                square = z * z
                r = lax.rsqrt(1.0 - square)
                carry = carry + jnp.sum(z * polynomial(square, LAST) + tangent * r, axis=0)
                slope = (2.0 * q * w9) * (uv * r)
                bent = tangent * (r * r)
                put(f3, row, c0, slope)
                put(f2, row, c0, slope * (2.0 + z * bent))
                keep(n3_ref, row, c0, r * (z + bent))
        return carry

    rows(pass_cross)
    rows(pass_first)
    rows(pass_second)
    mean = rows(pass_third, jnp.zeros((8, LANES), jnp.float32))
    kernel = (weight_variance * q / pixels) * mean + bias_variance

    part_ref[...] = jnp.dot(
        kernel, coeffs, precision=lax.Precision.HIGHEST,
        preferred_element_type=jnp.float32,
    )
    pl.semaphore_wait(barrier, n_sup - 1)
    copies = []
    for step in range(1, n_sup):
        copy = pltpu.make_async_remote_copy(
            src_ref=part_ref,
            dst_ref=arrived.at[step - 1],
            send_sem=send_sem.at[step - 1],
            recv_sem=recv_sem.at[step - 1],
            device_id={"sup": lax.rem(me + step, n_sup)},
            device_id_type=MESH,
        )
        copy.start()
        copies.append(copy)
    for copy in copies:
        copy.wait()
    predictions = part_ref[...]
    for step in range(n_sup - 1):
        predictions = predictions + arrived[step]
    pred_ref[...] = predictions
    target = lax.broadcasted_iota(jnp.int32, predictions.shape, 0)
    label = jnp.zeros(predictions.shape, jnp.int32)
    for k in range(8):
        label = jnp.where(target == k, label_ref[k], label)
    onehot = (label == lax.broadcasted_iota(jnp.int32, predictions.shape, 1)).astype(jnp.float32)
    error = loss_weight * (predictions - onehot)
    weights = lax.dot_general(
        error, coeffs, (((1,), (1,)), ((), ())), precision=lax.Precision.HIGHEST,
        preferred_element_type=jnp.float32,
    )
    kappa = (weight_variance / pixels) * weights

    sublane = lax.broadcasted_iota(jnp.int32, (8, LANES), 0)
    odd = [lax.rem(sublane // step, 2) == 1 for step in (1, 2, 4)]

    def total_rows(value):
        items = [value[j] for j in range(CHUNK)]
        for step, mask in zip((1, 2, 4), odd):
            items = [
                jnp.where(mask, second, first)
                + pltpu.roll(jnp.where(mask, first, second), step, 0)
                for first, second in zip(items[::2], items[1::2])
            ]
        return items[0]

    def pass_back_second(first, carry):
        for c0 in starts:
            pairs = zip((first, first + 1), box(f2, first, c0), box(f3, first, c0))
            for row, up, mean_up in pairs:
                uv = spread(u_ref, 1, row, c0) * across(vb_ref, 1, row, c0)
                z = kept(z2_ref, row, c0)
                r = kept(r2_ref, row, c0)
                up = kappa * up
                mean_up = kappa * mean_up
                bent = mean_up * kept(th2_ref, row, c0) * (r * r)
                slope = (2.0 * q * w9) * (uv * r)
                put(f4, row, c0, mean_up * slope)
                put(f1, row, c0, slope * (up + mean_up + bent * z))
                place = pl.ds(pl.multiple_of(row * SIDE + c0, CHUNK), CHUNK)
                nb_ref[4, place] = total_rows(r * (up * z + bent))
                nb_ref[5, place] = total_rows(kappa * kept(n3_ref, row, c0))
        return carry

    def pass_back_first(first, carry):
        for c0 in starts:
            pairs = zip((first, first + 1), box(f1, first, c0), box(f4, first, c0))
            for row, up, mean_up in pairs:
                uv = spread(u_ref, 0, row, c0) * across(vb_ref, 0, row, c0)
                r = kept(r1_ref, row, c0)
                joined = r * (up + (r * r) * mean_up)
                put(f2, row, c0, (2.0 * q * w9 / channels) * (uv * joined))
                place = pl.ds(pl.multiple_of(row * SIDE + c0, CHUNK), CHUNK)
                nb_ref[3, place] = total_rows(kept(z1_ref, row, c0) * joined)
        return carry

    rows(pass_back_second)
    rows(pass_back_first)

    def own_back(layer):
        source, target = (layer + 1) % 2, layer % 2

        def body(row, carry):
            n = nb_ref[layer, line(row)]
            b = 1.0 + 2.0 * n
            value = nb_ref[3 + layer, line(row)] * (-q / b)
            if layer < 2:
                value = value + (2.0 * w9 * q) * flat_box(source, row) * (
                    lax.rsqrt(1.0 + 4.0 * n) / b
                )
            sf_ref[target, line(row + 1)] = value
            return carry

        lax.fori_loop(0, SIDE, body, 0)

    for layer in (2, 1, 0):
        own_back(layer)

    def pass_images(first, carry):
        for row in (first, first + 1):
            own = (2.0 * w9 / channels) * flat_box(0, row)
            for c in range(channels):
                sum_ref[c, line(row)] = own * s_ref[c, line(row)]
        for c0 in starts:
            for row, value in zip((first, first + 1), box(f2, first, c0)):
                place = pl.ds(pl.multiple_of(row * SIDE + c0, CHUNK), CHUNK)
                for c in range(channels):
                    sum_ref[c, place] += total_rows(value * spread(t_ref, c, row, c0))
        return carry

    rows(pass_images)
    for c in range(channels):
        def turn(group, carry, c=c):
            place = pl.ds(pl.multiple_of(group * LANES, LANES), LANES)
            grad_ref[c * (pixels // LANES) + group] = jnp.transpose(sum_ref[c, place])
            return carry

        lax.fori_loop(0, pixels // LANES, turn, 0)


def tangent(s, targets, labels, dual_coeffs, n_sup):
    channels = s.shape[0]
    pixels = SIDE * SIDE
    classes = dual_coeffs.shape[2]
    field = pltpu.VMEM((SIDE + 2, SIDE + 2, 8, LANES), jnp.float32)
    plain = pltpu.VMEM((SIDE, SIDE, 8, LANES), jnp.float32)
    vmem = pl.BlockSpec(memory_space=pltpu.VMEM)
    return pl.pallas_call(
        functools.partial(tangent_body, n_sup, channels),
        out_shape=(
            jax.ShapeDtypeStruct((8, classes), jnp.float32),
            jax.ShapeDtypeStruct((channels * pixels // LANES, LANES, LANES), jnp.float32),
        ),
        in_specs=[vmem, vmem, pl.BlockSpec(memory_space=pltpu.SMEM), vmem],
        out_specs=(vmem, vmem),
        scratch_shapes=[field] * 4 + [plain] * 6 + [
            pltpu.VMEM((channels, SIDE, 8, LANES), jnp.float32),
            pltpu.VMEM((3, SIDE, 8, LANES), jnp.float32),
            pltpu.VMEM((channels, pixels, 1, LANES), jnp.float32),
            pltpu.VMEM((3, pixels, 1, LANES), jnp.float32),
            pltpu.VMEM((2, pixels + 2 * SIDE, LANES), jnp.float32),
            pltpu.VMEM((6, pixels, LANES), jnp.float32),
            pltpu.VMEM((channels, pixels, LANES), jnp.float32),
            pltpu.VMEM((8, classes), jnp.float32),
            pltpu.VMEM((n_sup - 1, 8, classes), jnp.float32),
            pltpu.SemaphoreType.DMA((n_sup - 1,)),
            pltpu.SemaphoreType.DMA((n_sup - 1,)),
        ],
        compiler_params=pltpu.CompilerParams(
            collective_id=1, has_side_effects=True, vmem_limit_bytes=60 << 20
        ),
        name="tangent_kernel",
    )(s, targets, labels, dual_coeffs)


def local(n_tgt, n_sup, targets, labels, support_slots, block_owner, dual_coeffs):
    blocks, per_block, _ = dual_coeffs.shape
    channels = targets.shape[1]
    pixels = targets.shape[2]
    supports = blocks * per_block
    if supports == LANES and (pixels * per_block) % (n_tgt * LANES * 8) == 0:
        s = gather(support_slots[0], block_owner, n_tgt)
    else:
        mine = block_owner == lax.axis_index("tgt")
        slot = jnp.transpose(support_slots[0], (1, 2, 0))
        own = jnp.where(mine[None, None, :, None], slot[:, :, None, :], 0.0)
        own = own.reshape(channels * pixels, supports)
        s = all_reduce(jnp.pad(own, ((0, 0), (0, LANES - supports))), n_tgt, 0)
    s = s.reshape(channels, pixels, LANES)

    predictions, grad = tangent(s, targets, labels, dual_coeffs, n_sup)
    grad = all_reduce(grad.reshape(channels * pixels, LANES), n_tgt, 2)
    grad = grad.reshape(channels, pixels // LANES, LANES, LANES)[:, :, :supports]
    grad = jnp.transpose(grad, (2, 0, 1, 3)).reshape(blocks, per_block, channels, pixels)
    return predictions, grad


def solution(mesh):
    return jax.shard_map(
        functools.partial(local, mesh.shape["tgt"], mesh.shape["sup"]),
        mesh=mesh,
        in_specs=(
            P("tgt", None, None),
            P("tgt"),
            P("tgt", "sup", None, None),
            P(),
            P(None, "sup", None),
        ),
        out_specs=(P("tgt", None), P(None, "sup", None, None)),
        check_vma=False,
    )
```

```python
import functools

import jax
import jax.numpy as jnp
from jax import lax
from jax.experimental import pallas as pl
from jax.experimental.pallas import tpu as pltpu
from jax.sharding import PartitionSpec as P

SIDE = 32
LANES = 128
CHUNK = 8
MESH = pl.DeviceIdType.MESH

weight_variance = 1.6
bias_variance = 0.1
loss_weight = 64.0
q = 2.0 / 3.141592653589793
w9 = weight_variance / 9.0

HALF = (
    0.9999998807907104, 0.16668881475925446, 0.07438822090625763,
    0.05069158226251602, 0.0044584982098147, 0.06837297230958939,
)
MIDDLE = (
    1.0000003576278687, 0.16661593317985535, 0.0763598307967186, 0.03124197944998741,
    0.09119893610477448, -0.11032058298587799, 0.1385442167520523,
)
LAST = (
    0.9999997615814209, 0.16670268774032593, 0.07408007979393005,
    0.0530407689511776, -0.0027404483407735825, 0.07600238919258118,
)


def polynomial(x, coefficients):
    total = jnp.full_like(x, coefficients[-1])
    for value in coefficients[-2::-1]:
        total = total * x + value
    return total


def wide_arcsin(z, complement, r):
    cosine = complement * r
    half = z * lax.rsqrt(2.0 + 2.0 * cosine)
    return (half + half) * polynomial(0.5 - 0.5 * cosine, HALF)


def stage_sizes(devices):
    bits = devices.bit_length() - 1
    low = max((bits - 1) // 2, 0)
    return [size for size in (min(devices, 2), 2 ** low, 2 ** (bits - 1 - low)) if size > 1]


class Stages:
    def __init__(self, sizes):
        self.sizes = sizes
        self.me = lax.axis_index("tgt")
        self.strides, self.digits = [], []
        stride = 1
        for size in sizes:
            self.strides.append(stride)
            self.digits.append(lax.rem(self.me // stride, size))
            stride = stride * size

    def place(self, device):
        total = 0
        for size, stride in zip(self.sizes, self.strides):
            total = total * size + lax.rem(device // stride, size)
        return total

    def peer(self, stage, step):
        digit = lax.rem(self.digits[stage] + step, self.sizes[stage])
        return digit, self.me + (digit - self.digits[stage]) * self.strides[stage]

    def base(self, stage, rows):
        total = 0
        for size, digit in zip(self.sizes[:stage + 1], self.digits):
            rows = rows // size
            total = total + digit * rows
        return total

    def back_copies(self, out_ref, piece, first, rows, stage, send, receive):
        held = rows
        for size in self.sizes[:stage + 1]:
            held = held // size
        place = pl.ds(pl.multiple_of(first + self.base(stage, rows), 8), held)
        before = sum(size - 1 for size in self.sizes[:stage])
        copies = []
        for step in range(1, self.sizes[stage]):
            copies.append(pltpu.make_async_remote_copy(
                src_ref=out_ref.at[place],
                dst_ref=out_ref.at[place],
                send_sem=send.at[piece, before + step - 1],
                recv_sem=receive.at[piece, before + step - 1],
                device_id={"tgt": self.peer(stage, step)[1]},
                device_id_type=MESH,
            ))
        return copies


def start_all(copies):
    for copy in copies:
        copy.start()
    return copies


def all_reduce_body(sizes, pieces, x_ref, out_ref, *scratch):
    stages = len(sizes)
    received = scratch[:stages]
    partial = scratch[stages:2 * stages - 1]
    send_sem, recv_sem, send_back, recv_back = scratch[2 * stages - 1:]
    where = Stages(sizes)
    barrier = pltpu.get_barrier_semaphore()
    for stage, size in enumerate(sizes):
        for step in range(1, size):
            pl.semaphore_signal(
                barrier, inc=1, device_id={"tgt": where.peer(stage, step)[1]},
                device_id_type=MESH,
            )
    pl.semaphore_wait(barrier, sum(size - 1 for size in sizes))
    rows = x_ref.shape[0] // pieces
    held = [rows]
    for size in sizes:
        held.append(held[-1] // size)

    def source(stage, piece):
        if stage == 0:
            return x_ref.at[pl.ds(piece * rows, rows)]
        return partial[stage - 1].at[piece]

    def send(stage, piece):
        size = sizes[stage]
        before = sum(other - 1 for other in sizes[:stage])
        copies = []
        for step in range(1, size):
            digit, device = where.peer(stage, step)
            part = pl.ds(pl.multiple_of(digit * held[stage + 1], 8), held[stage + 1])
            copies.append(pltpu.make_async_remote_copy(
                src_ref=source(stage, piece).at[part],
                dst_ref=received[stage].at[piece, step - 1],
                send_sem=send_sem.at[piece, before + step - 1],
                recv_sem=recv_sem.at[piece, before + step - 1],
                device_id={"tgt": device},
                device_id_type=MESH,
            ))
        return start_all(copies)

    def add(stage, piece, copies):
        part = pl.ds(
            pl.multiple_of(where.digits[stage] * held[stage + 1], 8), held[stage + 1]
        )
        total = source(stage, piece)[part]
        for copy in copies:
            copy.wait()
        for slot in range(sizes[stage] - 1):
            total = total + received[stage][piece, slot]
        if stage + 1 < stages:
            partial[stage][piece] = total
        else:
            place = pl.multiple_of(piece * rows + where.base(stage, rows), 8)
            out_ref[pl.ds(place, held[stage + 1])] = total

    def back(step, piece):
        return start_all(where.back_copies(
            out_ref, piece, piece * rows, rows, stages - 1 - step, send_back, recv_back
        ))

    pending = [send(0, piece) for piece in range(pieces)]
    for tick in range(pieces + 2 * stages - 1):
        for piece in range(pieces):
            level = tick - piece
            if level < 0 or level >= 2 * stages:
                continue
            if level < stages:
                add(level, piece, pending[piece])
            else:
                for copy in pending[piece]:
                    copy.wait()
            if level + 1 < stages:
                pending[piece] = send(level + 1, piece)
            elif level + 1 < 2 * stages:
                pending[piece] = back(level + 1 - stages, piece)


def all_reduce(x, devices, collective_id):
    sizes = stage_sizes(devices)
    pieces = max(k for k in (1, 2, 3) if x.shape[0] % (k * devices * 8) == 0)
    rows = x.shape[0] // pieces
    received, partial = [], []
    for size in sizes:
        rows = rows // size
        received.append(pltpu.VMEM((pieces, size - 1, rows, LANES), jnp.float32))
        partial.append(pltpu.VMEM((pieces, rows, LANES), jnp.float32))
    copies = sum(size - 1 for size in sizes)
    return pl.pallas_call(
        functools.partial(all_reduce_body, sizes, pieces),
        out_shape=jax.ShapeDtypeStruct(x.shape, x.dtype),
        in_specs=[pl.BlockSpec(memory_space=pltpu.VMEM)],
        out_specs=pl.BlockSpec(memory_space=pltpu.VMEM),
        scratch_shapes=received + partial[:-1] + [pltpu.SemaphoreType.DMA((pieces, copies))] * 4,
        compiler_params=pltpu.CompilerParams(
            collective_id=collective_id, has_side_effects=True, vmem_limit_bytes=24 << 20
        ),
        name="sum_over_targets",
    )(x)


def gather_body(devices, channels, blocks, owner_ref, x_ref, out_ref, *scratch):
    slots = scratch[:channels]
    send_sem, recv_sem, send_back, recv_back = scratch[channels:]
    sizes = stage_sizes(devices)
    stages = len(sizes)
    where = Stages(sizes)
    me = where.me
    barrier = pltpu.get_barrier_semaphore()
    for step in range(1, devices):
        pl.semaphore_signal(
            barrier, inc=1, device_id={"tgt": lax.rem(me + step, devices)}, device_id_type=MESH
        )
    pl.semaphore_wait(barrier, devices - 1)
    packed = x_ref.shape[1] // channels
    copies = []
    for c in range(channels):
        part = pl.ds(c * packed, packed)
        copies.append([])
        for step in range(1, devices):
            device = lax.rem(me + step, devices)
            copies[c].append(pltpu.make_async_remote_copy(
                src_ref=x_ref.at[where.place(device), part],
                dst_ref=slots[c].at[me],
                send_sem=send_sem.at[c, step - 1],
                recv_sem=recv_sem.at[c, step - 1],
                device_id={"tgt": device},
                device_id_type=MESH,
            ))
        start_all(copies[c])
    for c in range(channels):
        slots[c][me] = x_ref[where.place(me), pl.ds(c * packed, packed)]
    rows = out_ref.shape[0] // channels
    chunk = rows // devices
    groups = chunk // packed
    width = LANES // groups
    block = lax.broadcasted_iota(jnp.int32, (packed, LANES), 1) // width
    base = where.base(stages - 1, rows)
    pending = []
    for c in range(channels):
        for copy in copies[c]:
            copy.wait()
        parts = [slots[c][owner_ref[b]] for b in range(blocks)]
        for k in range(groups):
            total = jnp.zeros((packed, LANES), jnp.float32)
            for b in range(blocks):
                shift = (width * (b - k)) % LANES
                moved = pltpu.roll(parts[b], shift, 1) if shift else parts[b]
                total = jnp.where(block == b, moved, total)
            out_ref[pl.ds(pl.multiple_of(c * rows + base + k * packed, 8), packed)] = total
        pending.append(start_all(where.back_copies(
            out_ref, c, c * rows, rows, stages - 1, send_back, recv_back
        )))
    for tick in range(channels + stages - 1):
        for c in range(channels):
            level = tick - c
            if level < 0 or level >= stages:
                continue
            for copy in pending[c]:
                copy.wait()
            if level + 1 < stages:
                pending[c] = start_all(where.back_copies(
                    out_ref, c, c * rows, rows, stages - 2 - level, send_back, recv_back
                ))


def gather(slot, owner, devices):
    per_block, channels, pixels = slot.shape
    blocks = owner.shape[0]
    groups = LANES // per_block
    packed = pixels // devices // groups
    x = slot.reshape(per_block, channels, devices, groups, packed)
    x = jnp.transpose(x, (2, 1, 4, 3, 0)).reshape(devices, channels * packed, LANES)
    copies = sum(size - 1 for size in stage_sizes(devices))
    vmem = pl.BlockSpec(memory_space=pltpu.VMEM)
    return pl.pallas_call(
        functools.partial(gather_body, devices, channels, blocks),
        out_shape=jax.ShapeDtypeStruct((channels * pixels, LANES), jnp.float32),
        in_specs=[pl.BlockSpec(memory_space=pltpu.SMEM), vmem],
        out_specs=vmem,
        scratch_shapes=[pltpu.VMEM((devices, packed, LANES), jnp.float32)] * channels + [
            pltpu.SemaphoreType.DMA((channels, devices - 1)),
            pltpu.SemaphoreType.DMA((channels, devices - 1)),
            pltpu.SemaphoreType.DMA((channels, copies)),
            pltpu.SemaphoreType.DMA((channels, copies)),
        ],
        compiler_params=pltpu.CompilerParams(
            collective_id=0, has_side_effects=True, vmem_limit_bytes=24 << 20
        ),
        name="gather_supports",
    )(owner, x)


def tangent_body(
    n_sup, channels, s_ref, raw_ref, label_ref, dual_ref, pred_ref, grad_ref,
    f1, f2, f3, f4, z1_ref, r1_ref, z2_ref, r2_ref, th2_ref, n3_ref, t_ref, u_ref, sb_ref, vb_ref, sf_ref, nb_ref, sum_ref, part_ref,
    arrived, send_sem, recv_sem,
):
    pixels = SIDE * SIDE
    me = lax.axis_index("sup")
    barrier = pltpu.get_barrier_semaphore()
    for step in range(1, n_sup):
        pl.semaphore_signal(
            barrier, inc=1, device_id={"sup": lax.rem(me + step, n_sup)}, device_id_type=MESH
        )

    lane = lax.broadcasted_iota(jnp.int32, (8, LANES), 1)
    t_ref[...] = jnp.zeros(t_ref.shape, jnp.float32)
    for c in range(channels):
        image = raw_ref[:, c, :]
        for row in range(SIDE):
            t_ref[c, row, :, :SIDE] = image[:, row * SIDE:(row + 1) * SIDE]

    def lane_box(x):
        none = jnp.zeros((1, 8, LANES), jnp.float32)
        total = x + jnp.concatenate([none, x[:-1]]) + jnp.concatenate([x[1:], none])
        left = jnp.where(lane == 0, 0.0, pltpu.roll(total, 1, 2))
        right = jnp.where(lane == SIDE - 1, 0.0, pltpu.roll(total, LANES - 1, 2))
        return total + left + right

    power = t_ref[0] * t_ref[0]
    for c in range(1, channels):
        power = power + t_ref[c] * t_ref[c]
    n_t = (w9 / channels) * lane_box(power) + bias_variance
    for layer in range(3):
        b_t = 1.0 + 2.0 * n_t
        u_ref[layer] = lax.rsqrt(b_t)
        if layer < 2:
            z_t = 2.0 * n_t / b_t
            if layer == 0:
                rest = 1.0 - z_t * z_t
                angle_t = wide_arcsin(z_t, rest, lax.rsqrt(rest))
            else:
                angle_t = z_t * polynomial(z_t * z_t, MIDDLE)
            angle_t = jnp.where(lane < SIDE, angle_t, 0.0)
            n_t = (w9 * q) * lane_box(angle_t) + bias_variance

    for field in (f1, f2, f3, f4):
        for row in (0, SIDE + 1):
            field[row] = jnp.zeros(field.shape[1:], jnp.float32)

        def border(row, carry, field=field):
            for column in (0, SIDE + 1):
                field[row, column] = jnp.zeros(field.shape[2:], jnp.float32)
            return carry

        lax.fori_loop(1, SIDE + 1, border, 0)

    zero_row = jnp.zeros((SIDE, LANES), jnp.float32)
    for slot in range(2):
        sf_ref[slot, pl.ds(0, SIDE)] = zero_row
        sf_ref[slot, pl.ds(SIDE + pixels, SIDE)] = zero_row
    column = lax.broadcasted_iota(jnp.int32, (SIDE, LANES), 0)

    def line(row):
        return pl.ds(pl.multiple_of(row * SIDE, SIDE), SIDE)

    def flat_box(slot, row):
        x = (
            sf_ref[slot, line(row)] + sf_ref[slot, line(row + 1)] + sf_ref[slot, line(row + 2)]
        )
        left = jnp.where(column == 0, 0.0, pltpu.roll(x, 1, 0))
        right = jnp.where(column == SIDE - 1, 0.0, pltpu.roll(x, SIDE - 1, 0))
        return x + left + right

    def squares(row, carry):
        total = jnp.zeros((SIDE, LANES), jnp.float32)
        for c in range(channels):
            image = s_ref[c, line(row)]
            total = total + image * image
            for j in range(SIDE):
                sb_ref[c, row * SIDE + j] = image[j:j + 1]
        sf_ref[0, line(row + 1)] = total
        return carry

    lax.fori_loop(0, SIDE, squares, 0)

    def own_layer(layer):
        source, target = layer % 2, (layer + 1) % 2
        scale = w9 / channels if layer == 0 else w9 * q

        def body(row, carry):
            n = scale * flat_box(source, row) + bias_variance
            b = 1.0 + 2.0 * n
            v = lax.rsqrt(b)
            nb_ref[layer, line(row)] = n
            for j in range(SIDE):
                vb_ref[layer, row * SIDE + j] = v[j:j + 1]
            if layer < 2:
                z = 2.0 * n / b
                if layer == 0:
                    complement = 1.0 - z * z
                    angle = wide_arcsin(z, complement, lax.rsqrt(complement))
                else:
                    angle = z * polynomial(z * z, MIDDLE)
                sf_ref[target, line(row + 1)] = angle
            return carry

        lax.fori_loop(0, SIDE, body, 0)

    for layer in range(3):
        own_layer(layer)

    coeffs = dual_ref[...].reshape(-1, dual_ref.shape[2])
    if coeffs.shape[0] < LANES:
        coeffs = jnp.pad(coeffs, ((0, LANES - coeffs.shape[0]), (0, 0)))

    def rows(function, init=0):
        def four(step, carry):
            return function(step * 4 + 2, function(step * 4, carry))

        return lax.fori_loop(0, SIDE // 4, four, init)

    def spread(ref, k, row, c0):
        values = ref[k, row]
        return jnp.stack(
            [jnp.broadcast_to(values[:, c0 + j:c0 + j + 1], (8, LANES)) for j in range(CHUNK)]
        )

    def across(ref, k, row, c0):
        values = ref[k, pl.ds(row * SIDE + c0, CHUNK)]
        return jnp.broadcast_to(values, (CHUNK, 8, LANES))

    def box(ref, row, c0):
        lines = [ref[row + k, pl.ds(c0, CHUNK + 2)] for k in range(4)]
        middle = lines[1] + lines[2]
        sums = [lines[0] + middle, middle + lines[3]]
        return [x[:-2] + x[1:-1] + x[2:] for x in sums]

    def put(ref, row, c0, value):
        ref[row + 1, pl.ds(c0 + 1, CHUNK)] = value

    def keep(ref, row, c0, value):
        ref[row, pl.ds(c0, CHUNK)] = value

    def kept(ref, row, c0):
        return ref[row, pl.ds(c0, CHUNK)]

    starts = range(0, SIDE, CHUNK)

    def pass_cross(first, carry):
        for row in (first, first + 1):
            for c0 in starts:
                total = spread(t_ref, 0, row, c0) * across(sb_ref, 0, row, c0)
                for c in range(1, channels):
                    total = total + spread(t_ref, c, row, c0) * across(sb_ref, c, row, c0)
                put(f1, row, c0, total)
        return carry

    def pass_first(first, carry):
        for c0 in starts:
            for row, value in zip((first, first + 1), box(f1, first, c0)):
                uv = spread(u_ref, 0, row, c0) * across(vb_ref, 0, row, c0)
                z = uv * ((2.0 * w9 / channels) * value + 2.0 * bias_variance)
                complement = 1.0 - z * z
                r = lax.rsqrt(complement)
                keep(z1_ref, row, c0, z)
                keep(r1_ref, row, c0, r)
                put(f2, row, c0, wide_arcsin(z, complement, r))
                put(f3, row, c0, z * r)
        return carry

    def pass_second(first, carry):
        for c0 in starts:
            pairs = zip((first, first + 1), box(f2, first, c0), box(f3, first, c0))
            for row, angles, tangents in pairs:
                uv = spread(u_ref, 1, row, c0) * across(vb_ref, 1, row, c0)
                z = uv * ((2.0 * w9 * q) * angles + 2.0 * bias_variance)
                tangent = z + uv * ((2.0 * w9 * q) * tangents)
                square = z * z
                r = lax.rsqrt(1.0 - square)
                keep(z2_ref, row, c0, z)
                keep(r2_ref, row, c0, r)
                keep(th2_ref, row, c0, tangent)
                put(f1, row, c0, z * polynomial(square, MIDDLE))
                put(f4, row, c0, tangent * r)
        return carry

    def pass_third(first, carry):
        for c0 in starts:
            pairs = zip((first, first + 1), box(f1, first, c0), box(f4, first, c0))
            for row, angles, tangents in pairs:
                uv = spread(u_ref, 2, row, c0) * across(vb_ref, 2, row, c0)
                z = uv * ((2.0 * w9 * q) * angles + 2.0 * bias_variance)
                tangent = z + uv * ((2.0 * w9 * q) * tangents)
                square = z * z
                r = lax.rsqrt(1.0 - square)
                carry = carry + jnp.sum(z * polynomial(square, LAST) + tangent * r, axis=0)
                slope = (2.0 * q * w9) * (uv * r)
                bent = tangent * (r * r)
                put(f3, row, c0, slope)
                put(f2, row, c0, slope * (2.0 + z * bent))
                keep(n3_ref, row, c0, r * (z + bent))
        return carry

    rows(pass_cross)
    rows(pass_first)
    rows(pass_second)
    mean = rows(pass_third, jnp.zeros((8, LANES), jnp.float32))
    kernel = (weight_variance * q / pixels) * mean + bias_variance

    part_ref[...] = jnp.dot(
        kernel, coeffs, precision=lax.Precision.HIGHEST,
        preferred_element_type=jnp.float32,
    )
    pl.semaphore_wait(barrier, n_sup - 1)
    copies = []
    for step in range(1, n_sup):
        copy = pltpu.make_async_remote_copy(
            src_ref=part_ref,
            dst_ref=arrived.at[step - 1],
            send_sem=send_sem.at[step - 1],
            recv_sem=recv_sem.at[step - 1],
            device_id={"sup": lax.rem(me + step, n_sup)},
            device_id_type=MESH,
        )
        copy.start()
        copies.append(copy)
    for copy in copies:
        copy.wait()
    predictions = part_ref[...]
    for step in range(n_sup - 1):
        predictions = predictions + arrived[step]
    pred_ref[...] = predictions
    target = lax.broadcasted_iota(jnp.int32, predictions.shape, 0)
    label = jnp.zeros(predictions.shape, jnp.int32)
    for k in range(8):
        label = jnp.where(target == k, label_ref[k], label)
    onehot = (label == lax.broadcasted_iota(jnp.int32, predictions.shape, 1)).astype(jnp.float32)
    error = loss_weight * (predictions - onehot)
    weights = lax.dot_general(
        error, coeffs, (((1,), (1,)), ((), ())), precision=lax.Precision.HIGHEST,
        preferred_element_type=jnp.float32,
    )
    kappa = (weight_variance / pixels) * weights

    sublane = lax.broadcasted_iota(jnp.int32, (8, LANES), 0)
    odd = [lax.rem(sublane // step, 2) == 1 for step in (1, 2, 4)]

    def total_rows(value):
        items = [value[j] for j in range(CHUNK)]
        for step, mask in zip((1, 2, 4), odd):
            items = [
                jnp.where(mask, second, first)
                + pltpu.roll(jnp.where(mask, first, second), step, 0)
                for first, second in zip(items[::2], items[1::2])
            ]
        return items[0]

    def pass_back_second(first, carry):
        for c0 in starts:
            pairs = zip((first, first + 1), box(f2, first, c0), box(f3, first, c0))
            for row, up, mean_up in pairs:
                uv = spread(u_ref, 1, row, c0) * across(vb_ref, 1, row, c0)
                z = kept(z2_ref, row, c0)
                r = kept(r2_ref, row, c0)
                up = kappa * up
                mean_up = kappa * mean_up
                bent = mean_up * kept(th2_ref, row, c0) * (r * r)
                slope = (2.0 * q * w9) * (uv * r)
                put(f4, row, c0, mean_up * slope)
                put(f1, row, c0, slope * (up + mean_up + bent * z))
                place = pl.ds(pl.multiple_of(row * SIDE + c0, CHUNK), CHUNK)
                nb_ref[4, place] = total_rows(r * (up * z + bent))
                nb_ref[5, place] = total_rows(kappa * kept(n3_ref, row, c0))
        return carry

    def pass_back_first(first, carry):
        for c0 in starts:
            pairs = zip((first, first + 1), box(f1, first, c0), box(f4, first, c0))
            for row, up, mean_up in pairs:
                uv = spread(u_ref, 0, row, c0) * across(vb_ref, 0, row, c0)
                r = kept(r1_ref, row, c0)
                joined = r * (up + (r * r) * mean_up)
                put(f2, row, c0, (2.0 * q * w9 / channels) * (uv * joined))
                place = pl.ds(pl.multiple_of(row * SIDE + c0, CHUNK), CHUNK)
                nb_ref[3, place] = total_rows(kept(z1_ref, row, c0) * joined)
        return carry

    rows(pass_back_second)
    rows(pass_back_first)

    def own_back(layer):
        source, target = (layer + 1) % 2, layer % 2

        def body(row, carry):
            n = nb_ref[layer, line(row)]
            b = 1.0 + 2.0 * n
            value = nb_ref[3 + layer, line(row)] * (-q / b)
            if layer < 2:
                value = value + (2.0 * w9 * q) * flat_box(source, row) * (
                    lax.rsqrt(1.0 + 4.0 * n) / b
                )
            sf_ref[target, line(row + 1)] = value
            return carry

        lax.fori_loop(0, SIDE, body, 0)

    for layer in (2, 1, 0):
        own_back(layer)

    def pass_images(first, carry):
        for row in (first, first + 1):
            own = (2.0 * w9 / channels) * flat_box(0, row)
            for c in range(channels):
                sum_ref[c, line(row)] = own * s_ref[c, line(row)]
        for c0 in starts:
            for row, value in zip((first, first + 1), box(f2, first, c0)):
                place = pl.ds(pl.multiple_of(row * SIDE + c0, CHUNK), CHUNK)
                for c in range(channels):
                    sum_ref[c, place] += total_rows(value * spread(t_ref, c, row, c0))
        return carry

    rows(pass_images)
    for c in range(channels):
        def turn(group, carry, c=c):
            place = pl.ds(pl.multiple_of(group * LANES, LANES), LANES)
            grad_ref[c * (pixels // LANES) + group] = jnp.transpose(sum_ref[c, place])
            return carry

        lax.fori_loop(0, pixels // LANES, turn, 0)


def tangent(s, targets, labels, dual_coeffs, n_sup):
    channels = s.shape[0]
    pixels = SIDE * SIDE
    classes = dual_coeffs.shape[2]
    field = pltpu.VMEM((SIDE + 2, SIDE + 2, 8, LANES), jnp.float32)
    plain = pltpu.VMEM((SIDE, SIDE, 8, LANES), jnp.float32)
    vmem = pl.BlockSpec(memory_space=pltpu.VMEM)
    return pl.pallas_call(
        functools.partial(tangent_body, n_sup, channels),
        out_shape=(
            jax.ShapeDtypeStruct((8, classes), jnp.float32),
            jax.ShapeDtypeStruct((channels * pixels // LANES, LANES, LANES), jnp.float32),
        ),
        in_specs=[vmem, vmem, pl.BlockSpec(memory_space=pltpu.SMEM), vmem],
        out_specs=(vmem, vmem),
        scratch_shapes=[field] * 4 + [plain] * 6 + [
            pltpu.VMEM((channels, SIDE, 8, LANES), jnp.float32),
            pltpu.VMEM((3, SIDE, 8, LANES), jnp.float32),
            pltpu.VMEM((channels, pixels, 1, LANES), jnp.float32),
            pltpu.VMEM((3, pixels, 1, LANES), jnp.float32),
            pltpu.VMEM((2, pixels + 2 * SIDE, LANES), jnp.float32),
            pltpu.VMEM((6, pixels, LANES), jnp.float32),
            pltpu.VMEM((channels, pixels, LANES), jnp.float32),
            pltpu.VMEM((8, classes), jnp.float32),
            pltpu.VMEM((n_sup - 1, 8, classes), jnp.float32),
            pltpu.SemaphoreType.DMA((n_sup - 1,)),
            pltpu.SemaphoreType.DMA((n_sup - 1,)),
        ],
        compiler_params=pltpu.CompilerParams(
            collective_id=1, has_side_effects=True, vmem_limit_bytes=60 << 20
        ),
        name="tangent_kernel",
    )(s, targets, labels, dual_coeffs)


def local(n_tgt, n_sup, targets, labels, support_slots, block_owner, dual_coeffs):
    blocks, per_block, _ = dual_coeffs.shape
    channels = targets.shape[1]
    pixels = targets.shape[2]
    supports = blocks * per_block
    if supports == LANES and (pixels * per_block) % (n_tgt * LANES * 8) == 0:
        s = gather(support_slots[0], block_owner, n_tgt)
    else:
        mine = block_owner == lax.axis_index("tgt")
        slot = jnp.transpose(support_slots[0], (1, 2, 0))
        own = jnp.where(mine[None, None, :, None], slot[:, :, None, :], 0.0)
        own = own.reshape(channels * pixels, supports)
        s = all_reduce(jnp.pad(own, ((0, 0), (0, LANES - supports))), n_tgt, 0)
    s = s.reshape(channels, pixels, LANES)

    predictions, grad = tangent(s, targets, labels, dual_coeffs, n_sup)
    grad = all_reduce(grad.reshape(channels * pixels, LANES), n_tgt, 2)
    grad = grad.reshape(channels, pixels // LANES, LANES, LANES)[:, :, :supports]
    grad = jnp.transpose(grad, (2, 0, 1, 3)).reshape(blocks, per_block, channels, pixels)
    return predictions, grad


def solution(mesh):
    return jax.shard_map(
        functools.partial(local, mesh.shape["tgt"], mesh.shape["sup"]),
        mesh=mesh,
        in_specs=(
            P("tgt", None, None),
            P("tgt"),
            P("tgt", "sup", None, None),
            P(),
            P(None, "sup", None),
        ),
        out_specs=(P("tgt", None), P(None, "sup", None, None)),
        check_vma=False,
    )
```

```python
import functools

import jax
import jax.numpy as jnp
from jax import lax
from jax.experimental import pallas as pl
from jax.experimental.pallas import tpu as pltpu
from jax.sharding import PartitionSpec as P

SIDE = 32
LANES = 128
CHUNK = 8
MESH = pl.DeviceIdType.MESH

weight_variance = 1.6
bias_variance = 0.1
loss_weight = 64.0
q = 2.0 / 3.141592653589793
w9 = weight_variance / 9.0

HALF = (
    0.9999998807907104, 0.16668881475925446, 0.07438822090625763,
    0.05069158226251602, 0.0044584982098147, 0.06837297230958939,
)
MIDDLE = (
    1.0000003576278687, 0.16661593317985535, 0.0763598307967186, 0.03124197944998741,
    0.09119893610477448, -0.11032058298587799, 0.1385442167520523,
)
LAST = (
    0.9999997615814209, 0.16670268774032593, 0.07408007979393005,
    0.0530407689511776, -0.0027404483407735825, 0.07600238919258118,
)


def polynomial(x, coefficients):
    total = jnp.full_like(x, coefficients[-1])
    for value in coefficients[-2::-1]:
        total = total * x + value
    return total


def wide_arcsin(z, complement, r):
    cosine = complement * r
    half = z * lax.rsqrt(2.0 + 2.0 * cosine)
    return (half + half) * polynomial(0.5 - 0.5 * cosine, HALF)


def stage_sizes(devices):
    bits = devices.bit_length() - 1
    low = max((bits - 1) // 2, 0)
    return [size for size in (min(devices, 2), 2 ** low, 2 ** (bits - 1 - low)) if size > 1]


class Stages:
    def __init__(self, sizes):
        self.sizes = sizes
        self.me = lax.axis_index("tgt")
        self.strides, self.digits = [], []
        stride = 1
        for size in sizes:
            self.strides.append(stride)
            self.digits.append(lax.rem(self.me // stride, size))
            stride = stride * size

    def place(self, device):
        total = 0
        for size, stride in zip(self.sizes, self.strides):
            total = total * size + lax.rem(device // stride, size)
        return total

    def peer(self, stage, step):
        digit = lax.rem(self.digits[stage] + step, self.sizes[stage])
        return digit, self.me + (digit - self.digits[stage]) * self.strides[stage]

    def base(self, stage, rows):
        total = 0
        for size, digit in zip(self.sizes[:stage + 1], self.digits):
            rows = rows // size
            total = total + digit * rows
        return total

    def back_copies(self, out_ref, piece, first, rows, stage, send, receive):
        held = rows
        for size in self.sizes[:stage + 1]:
            held = held // size
        place = pl.ds(pl.multiple_of(first + self.base(stage, rows), 8), held)
        before = sum(size - 1 for size in self.sizes[:stage])
        copies = []
        for step in range(1, self.sizes[stage]):
            copies.append(pltpu.make_async_remote_copy(
                src_ref=out_ref.at[place],
                dst_ref=out_ref.at[place],
                send_sem=send.at[piece, before + step - 1],
                recv_sem=receive.at[piece, before + step - 1],
                device_id={"tgt": self.peer(stage, step)[1]},
                device_id_type=MESH,
            ))
        return copies


def start_all(copies):
    for copy in copies:
        copy.start()
    return copies


def all_reduce_body(sizes, pieces, greet, x_ref, out_ref, *scratch):
    stages = len(sizes)
    received = scratch[:stages]
    partial = scratch[stages:2 * stages - 1]
    send_sem, recv_sem, send_back, recv_back = scratch[2 * stages - 1:]
    where = Stages(sizes)
    if greet:
        barrier = pltpu.get_barrier_semaphore()
        for stage, size in enumerate(sizes):
            for step in range(1, size):
                pl.semaphore_signal(
                    barrier, inc=1, device_id={"tgt": where.peer(stage, step)[1]},
                    device_id_type=MESH,
                )
        pl.semaphore_wait(barrier, sum(size - 1 for size in sizes))
    rows = x_ref.shape[0] // pieces
    held = [rows]
    for size in sizes:
        held.append(held[-1] // size)

    def source(stage, piece):
        if stage == 0:
            return x_ref.at[pl.ds(piece * rows, rows)]
        return partial[stage - 1].at[piece]

    def send(stage, piece):
        size = sizes[stage]
        before = sum(other - 1 for other in sizes[:stage])
        copies = []
        for step in range(1, size):
            digit, device = where.peer(stage, step)
            part = pl.ds(pl.multiple_of(digit * held[stage + 1], 8), held[stage + 1])
            copies.append(pltpu.make_async_remote_copy(
                src_ref=source(stage, piece).at[part],
                dst_ref=received[stage].at[piece, step - 1],
                send_sem=send_sem.at[piece, before + step - 1],
                recv_sem=recv_sem.at[piece, before + step - 1],
                device_id={"tgt": device},
                device_id_type=MESH,
            ))
        return start_all(copies)

    def add(stage, piece, copies):
        part = pl.ds(
            pl.multiple_of(where.digits[stage] * held[stage + 1], 8), held[stage + 1]
        )
        total = source(stage, piece)[part]
        for copy in copies:
            copy.wait()
        for slot in range(sizes[stage] - 1):
            total = total + received[stage][piece, slot]
        if stage + 1 < stages:
            partial[stage][piece] = total
        else:
            place = pl.multiple_of(piece * rows + where.base(stage, rows), 8)
            out_ref[pl.ds(place, held[stage + 1])] = total

    def back(step, piece):
        return start_all(where.back_copies(
            out_ref, piece, piece * rows, rows, stages - 1 - step, send_back, recv_back
        ))

    pending = [send(0, piece) for piece in range(pieces)]
    for tick in range(pieces + 2 * stages - 1):
        for piece in range(pieces):
            level = tick - piece
            if level < 0 or level >= 2 * stages:
                continue
            if level < stages:
                add(level, piece, pending[piece])
            else:
                for copy in pending[piece]:
                    copy.wait()
            if level + 1 < stages:
                pending[piece] = send(level + 1, piece)
            elif level + 1 < 2 * stages:
                pending[piece] = back(level + 1 - stages, piece)


def all_reduce_scratch(rows, devices):
    sizes = stage_sizes(devices)
    pieces = max(k for k in (1, 2, 3) if rows % (k * devices * 8) == 0)
    rows = rows // pieces
    received, partial = [], []
    for size in sizes:
        rows = rows // size
        received.append(pltpu.VMEM((pieces, size - 1, rows, LANES), jnp.float32))
        partial.append(pltpu.VMEM((pieces, rows, LANES), jnp.float32))
    copies = sum(size - 1 for size in sizes)
    semaphores = [pltpu.SemaphoreType.DMA((pieces, copies))] * 4
    return sizes, pieces, received + partial[:-1] + semaphores


def all_reduce(x, devices, collective_id):
    sizes, pieces, scratch = all_reduce_scratch(x.shape[0], devices)
    return pl.pallas_call(
        functools.partial(all_reduce_body, sizes, pieces, True),
        out_shape=jax.ShapeDtypeStruct(x.shape, x.dtype),
        in_specs=[pl.BlockSpec(memory_space=pltpu.VMEM)],
        out_specs=pl.BlockSpec(memory_space=pltpu.VMEM),
        scratch_shapes=scratch,
        compiler_params=pltpu.CompilerParams(
            collective_id=collective_id, has_side_effects=True, vmem_limit_bytes=24 << 20
        ),
        name="sum_over_targets",
    )(x)


def gather_body(devices, channels, blocks, meanwhile, owner_ref, x_ref, out_ref, *scratch):
    slots = scratch[:channels]
    send_sem, recv_sem, send_back, recv_back = scratch[channels:]
    sizes = stage_sizes(devices)
    stages = len(sizes)
    where = Stages(sizes)
    me = where.me
    packed = x_ref.shape[1] // channels
    copies = []
    for c in range(channels):
        part = pl.ds(c * packed, packed)
        copies.append([])
        for step in range(1, devices):
            device = lax.rem(me + step, devices)
            copies[c].append(pltpu.make_async_remote_copy(
                src_ref=x_ref.at[where.place(device), part],
                dst_ref=slots[c].at[me],
                send_sem=send_sem.at[c, step - 1],
                recv_sem=recv_sem.at[c, step - 1],
                device_id={"tgt": device},
                device_id_type=MESH,
            ))
        start_all(copies[c])
    for c in range(channels):
        slots[c][me] = x_ref[where.place(me), pl.ds(c * packed, packed)]
    meanwhile()
    rows = out_ref.shape[0] // channels
    chunk = rows // devices
    groups = chunk // packed
    width = LANES // groups
    block = lax.broadcasted_iota(jnp.int32, (packed, LANES), 1) // width
    base = where.base(stages - 1, rows)
    pending = []
    for c in range(channels):
        for copy in copies[c]:
            copy.wait()
        parts = [slots[c][owner_ref[b]] for b in range(blocks)]
        for k in range(groups):
            total = jnp.zeros((packed, LANES), jnp.float32)
            for b in range(blocks):
                shift = (width * (b - k)) % LANES
                moved = pltpu.roll(parts[b], shift, 1) if shift else parts[b]
                total = jnp.where(block == b, moved, total)
            out_ref[pl.ds(pl.multiple_of(c * rows + base + k * packed, 8), packed)] = total
        pending.append(start_all(where.back_copies(
            out_ref, c, c * rows, rows, stages - 1, send_back, recv_back
        )))
    for tick in range(channels + stages - 1):
        for c in range(channels):
            level = tick - c
            if level < 0 or level >= stages:
                continue
            for copy in pending[c]:
                copy.wait()
            if level + 1 < stages:
                pending[c] = start_all(where.back_copies(
                    out_ref, c, c * rows, rows, stages - 2 - level, send_back, recv_back
                ))


def pack_slot(slot, devices):
    per_block, channels, pixels = slot.shape
    groups = LANES // per_block
    packed = pixels // devices // groups
    x = slot.reshape(per_block, channels, devices, groups, packed)
    return jnp.transpose(x, (2, 1, 4, 3, 0)).reshape(devices, channels * packed, LANES)


def gather_scratch(packed_shape, channels, devices):
    _, rows, _ = packed_shape
    copies = sum(size - 1 for size in stage_sizes(devices))
    return [pltpu.VMEM((devices, rows // channels, LANES), jnp.float32)] * channels + [
        pltpu.SemaphoreType.DMA((channels, devices - 1)),
        pltpu.SemaphoreType.DMA((channels, devices - 1)),
        pltpu.SemaphoreType.DMA((channels, copies)),
        pltpu.SemaphoreType.DMA((channels, copies)),
    ]


def tangent_body(
    bring, n_sup, channels, s_ref, raw_ref, label_ref, dual_ref, pred_ref, grad_ref,
    f1, f2, f3, f4, z1_ref, r1_ref, z2_ref, r2_ref, th2_ref, n3_ref, t_ref, u_ref, sb_ref,
    vb_ref, sf_ref, nb_ref, sum_ref, part_ref, arrived, send_sem, recv_sem,
):
    pixels = SIDE * SIDE
    me = lax.axis_index("sup")

    def prepare():
        lane = lax.broadcasted_iota(jnp.int32, (8, LANES), 1)
        t_ref[...] = jnp.zeros(t_ref.shape, jnp.float32)
        for c in range(channels):
            image = raw_ref[:, c, :]
            for row in range(SIDE):
                t_ref[c, row, :, :SIDE] = image[:, row * SIDE:(row + 1) * SIDE]

        def lane_box(x):
            none = jnp.zeros((1, 8, LANES), jnp.float32)
            total = x + jnp.concatenate([none, x[:-1]]) + jnp.concatenate([x[1:], none])
            left = jnp.where(lane == 0, 0.0, pltpu.roll(total, 1, 2))
            right = jnp.where(lane == SIDE - 1, 0.0, pltpu.roll(total, LANES - 1, 2))
            return total + left + right

        power = t_ref[0] * t_ref[0]
        for c in range(1, channels):
            power = power + t_ref[c] * t_ref[c]
        n_t = (w9 / channels) * lane_box(power) + bias_variance
        for layer in range(3):
            b_t = 1.0 + 2.0 * n_t
            u_ref[layer] = lax.rsqrt(b_t)
            if layer < 2:
                z_t = 2.0 * n_t / b_t
                if layer == 0:
                    rest = 1.0 - z_t * z_t
                    angle_t = wide_arcsin(z_t, rest, lax.rsqrt(rest))
                else:
                    angle_t = z_t * polynomial(z_t * z_t, MIDDLE)
                angle_t = jnp.where(lane < SIDE, angle_t, 0.0)
                n_t = (w9 * q) * lane_box(angle_t) + bias_variance

        for field in (f1, f2, f3, f4):
            for row in (0, SIDE + 1):
                field[row] = jnp.zeros(field.shape[1:], jnp.float32)

            def border(row, carry, field=field):
                for column in (0, SIDE + 1):
                    field[row, column] = jnp.zeros(field.shape[2:], jnp.float32)
                return carry

            lax.fori_loop(1, SIDE + 1, border, 0)

    bring(prepare)

    zero_row = jnp.zeros((SIDE, LANES), jnp.float32)
    for slot in range(2):
        sf_ref[slot, pl.ds(0, SIDE)] = zero_row
        sf_ref[slot, pl.ds(SIDE + pixels, SIDE)] = zero_row
    column = lax.broadcasted_iota(jnp.int32, (SIDE, LANES), 0)

    def line(row):
        return pl.ds(pl.multiple_of(row * SIDE, SIDE), SIDE)

    def flat_box(slot, row):
        x = (
            sf_ref[slot, line(row)] + sf_ref[slot, line(row + 1)] + sf_ref[slot, line(row + 2)]
        )
        left = jnp.where(column == 0, 0.0, pltpu.roll(x, 1, 0))
        right = jnp.where(column == SIDE - 1, 0.0, pltpu.roll(x, SIDE - 1, 0))
        return x + left + right

    def squares(row, carry):
        total = jnp.zeros((SIDE, LANES), jnp.float32)
        for c in range(channels):
            image = s_ref[pl.ds(pl.multiple_of(c * pixels + row * SIDE, SIDE), SIDE)]
            total = total + image * image
            for j in range(SIDE):
                sb_ref[c, row * SIDE + j] = image[j:j + 1]
        sf_ref[0, line(row + 1)] = total
        return carry

    lax.fori_loop(0, SIDE, squares, 0)

    def own_layer(layer):
        source, target = layer % 2, (layer + 1) % 2
        scale = w9 / channels if layer == 0 else w9 * q

        def body(row, carry):
            n = scale * flat_box(source, row) + bias_variance
            b = 1.0 + 2.0 * n
            v = lax.rsqrt(b)
            nb_ref[layer, line(row)] = n
            for j in range(SIDE):
                vb_ref[layer, row * SIDE + j] = v[j:j + 1]
            if layer < 2:
                z = 2.0 * n / b
                if layer == 0:
                    complement = 1.0 - z * z
                    angle = wide_arcsin(z, complement, lax.rsqrt(complement))
                else:
                    angle = z * polynomial(z * z, MIDDLE)
                sf_ref[target, line(row + 1)] = angle
            return carry

        lax.fori_loop(0, SIDE, body, 0)

    for layer in range(3):
        own_layer(layer)

    coeffs = dual_ref[...].reshape(-1, dual_ref.shape[2])
    if coeffs.shape[0] < LANES:
        coeffs = jnp.pad(coeffs, ((0, LANES - coeffs.shape[0]), (0, 0)))

    def rows(function, init=0):
        def four(step, carry):
            return function(step * 4 + 2, function(step * 4, carry))

        return lax.fori_loop(0, SIDE // 4, four, init)

    def spread(ref, k, row, c0):
        values = ref[k, row]
        return jnp.stack(
            [jnp.broadcast_to(values[:, c0 + j:c0 + j + 1], (8, LANES)) for j in range(CHUNK)]
        )

    def across(ref, k, row, c0):
        values = ref[k, pl.ds(row * SIDE + c0, CHUNK)]
        return jnp.broadcast_to(values, (CHUNK, 8, LANES))

    def box(ref, row, c0):
        lines = [ref[row + k, pl.ds(c0, CHUNK + 2)] for k in range(4)]
        middle = lines[1] + lines[2]
        sums = [lines[0] + middle, middle + lines[3]]
        return [x[:-2] + x[1:-1] + x[2:] for x in sums]

    def put(ref, row, c0, value):
        ref[row + 1, pl.ds(c0 + 1, CHUNK)] = value

    def keep(ref, row, c0, value):
        ref[row, pl.ds(c0, CHUNK)] = value

    def kept(ref, row, c0):
        return ref[row, pl.ds(c0, CHUNK)]

    starts = range(0, SIDE, CHUNK)

    def pass_cross(first, carry):
        for row in (first, first + 1):
            for c0 in starts:
                total = spread(t_ref, 0, row, c0) * across(sb_ref, 0, row, c0)
                for c in range(1, channels):
                    total = total + spread(t_ref, c, row, c0) * across(sb_ref, c, row, c0)
                put(f1, row, c0, total)
        return carry

    def pass_first(first, carry):
        for c0 in starts:
            for row, value in zip((first, first + 1), box(f1, first, c0)):
                uv = spread(u_ref, 0, row, c0) * across(vb_ref, 0, row, c0)
                z = uv * ((2.0 * w9 / channels) * value + 2.0 * bias_variance)
                complement = 1.0 - z * z
                r = lax.rsqrt(complement)
                keep(z1_ref, row, c0, z)
                keep(r1_ref, row, c0, r)
                put(f2, row, c0, wide_arcsin(z, complement, r))
                put(f3, row, c0, z * r)
        return carry

    def pass_second(first, carry):
        for c0 in starts:
            pairs = zip((first, first + 1), box(f2, first, c0), box(f3, first, c0))
            for row, angles, tangents in pairs:
                uv = spread(u_ref, 1, row, c0) * across(vb_ref, 1, row, c0)
                z = uv * ((2.0 * w9 * q) * angles + 2.0 * bias_variance)
                tangent = z + uv * ((2.0 * w9 * q) * tangents)
                square = z * z
                r = lax.rsqrt(1.0 - square)
                keep(z2_ref, row, c0, z)
                keep(r2_ref, row, c0, r)
                keep(th2_ref, row, c0, tangent)
                put(f1, row, c0, z * polynomial(square, MIDDLE))
                put(f4, row, c0, tangent * r)
        return carry

    def pass_third(first, carry):
        for c0 in starts:
            pairs = zip((first, first + 1), box(f1, first, c0), box(f4, first, c0))
            for row, angles, tangents in pairs:
                uv = spread(u_ref, 2, row, c0) * across(vb_ref, 2, row, c0)
                z = uv * ((2.0 * w9 * q) * angles + 2.0 * bias_variance)
                tangent = z + uv * ((2.0 * w9 * q) * tangents)
                square = z * z
                r = lax.rsqrt(1.0 - square)
                carry = carry + jnp.sum(z * polynomial(square, LAST) + tangent * r, axis=0)
                slope = (2.0 * q * w9) * (uv * r)
                bent = tangent * (r * r)
                put(f3, row, c0, slope)
                put(f2, row, c0, slope * (2.0 + z * bent))
                keep(n3_ref, row, c0, r * (z + bent))
        return carry

    rows(pass_cross)
    rows(pass_first)
    rows(pass_second)
    mean = rows(pass_third, jnp.zeros((8, LANES), jnp.float32))
    kernel = (weight_variance * q / pixels) * mean + bias_variance

    part_ref[...] = jnp.dot(
        kernel, coeffs, precision=lax.Precision.HIGHEST,
        preferred_element_type=jnp.float32,
    )
    copies = []
    for step in range(1, n_sup):
        copy = pltpu.make_async_remote_copy(
            src_ref=part_ref,
            dst_ref=arrived.at[step - 1],
            send_sem=send_sem.at[step - 1],
            recv_sem=recv_sem.at[step - 1],
            device_id={"sup": lax.rem(me + step, n_sup)},
            device_id_type=MESH,
        )
        copy.start()
        copies.append(copy)
    for copy in copies:
        copy.wait()
    predictions = part_ref[...]
    for step in range(n_sup - 1):
        predictions = predictions + arrived[step]
    pred_ref[...] = predictions
    target = lax.broadcasted_iota(jnp.int32, predictions.shape, 0)
    label = jnp.zeros(predictions.shape, jnp.int32)
    for k in range(8):
        label = jnp.where(target == k, label_ref[k], label)
    onehot = (label == lax.broadcasted_iota(jnp.int32, predictions.shape, 1)).astype(jnp.float32)
    error = loss_weight * (predictions - onehot)
    weights = lax.dot_general(
        error, coeffs, (((1,), (1,)), ((), ())), precision=lax.Precision.HIGHEST,
        preferred_element_type=jnp.float32,
    )
    kappa = (weight_variance / pixels) * weights

    sublane = lax.broadcasted_iota(jnp.int32, (8, LANES), 0)
    odd = [lax.rem(sublane // step, 2) == 1 for step in (1, 2, 4)]

    def total_rows(value):
        items = [value[j] for j in range(CHUNK)]
        for step, mask in zip((1, 2, 4), odd):
            items = [
                jnp.where(mask, second, first)
                + pltpu.roll(jnp.where(mask, first, second), step, 0)
                for first, second in zip(items[::2], items[1::2])
            ]
        return items[0]

    def pass_back_second(first, carry):
        for c0 in starts:
            pairs = zip((first, first + 1), box(f2, first, c0), box(f3, first, c0))
            for row, up, mean_up in pairs:
                uv = spread(u_ref, 1, row, c0) * across(vb_ref, 1, row, c0)
                z = kept(z2_ref, row, c0)
                r = kept(r2_ref, row, c0)
                up = kappa * up
                mean_up = kappa * mean_up
                bent = mean_up * kept(th2_ref, row, c0) * (r * r)
                slope = (2.0 * q * w9) * (uv * r)
                put(f4, row, c0, mean_up * slope)
                put(f1, row, c0, slope * (up + mean_up + bent * z))
                place = pl.ds(pl.multiple_of(row * SIDE + c0, CHUNK), CHUNK)
                nb_ref[4, place] = total_rows(r * (up * z + bent))
                nb_ref[5, place] = total_rows(kappa * kept(n3_ref, row, c0))
        return carry

    def pass_back_first(first, carry):
        for c0 in starts:
            pairs = zip((first, first + 1), box(f1, first, c0), box(f4, first, c0))
            for row, up, mean_up in pairs:
                uv = spread(u_ref, 0, row, c0) * across(vb_ref, 0, row, c0)
                r = kept(r1_ref, row, c0)
                joined = r * (up + (r * r) * mean_up)
                put(f2, row, c0, (2.0 * q * w9 / channels) * (uv * joined))
                place = pl.ds(pl.multiple_of(row * SIDE + c0, CHUNK), CHUNK)
                nb_ref[3, place] = total_rows(kept(z1_ref, row, c0) * joined)
        return carry

    rows(pass_back_second)
    rows(pass_back_first)

    def own_back(layer):
        source, target = (layer + 1) % 2, layer % 2

        def body(row, carry):
            n = nb_ref[layer, line(row)]
            b = 1.0 + 2.0 * n
            value = nb_ref[3 + layer, line(row)] * (-q / b)
            if layer < 2:
                value = value + (2.0 * w9 * q) * flat_box(source, row) * (
                    lax.rsqrt(1.0 + 4.0 * n) / b
                )
            sf_ref[target, line(row + 1)] = value
            return carry

        lax.fori_loop(0, SIDE, body, 0)

    for layer in (2, 1, 0):
        own_back(layer)

    def pass_images(first, carry):
        for row in (first, first + 1):
            own = (2.0 * w9 / channels) * flat_box(0, row)
            for c in range(channels):
                sum_ref[c, line(row)] = own * s_ref[pl.ds(pl.multiple_of(c * pixels + row * SIDE, SIDE), SIDE)]
        for c0 in starts:
            for row, value in zip((first, first + 1), box(f2, first, c0)):
                place = pl.ds(pl.multiple_of(row * SIDE + c0, CHUNK), CHUNK)
                for c in range(channels):
                    sum_ref[c, place] += total_rows(value * spread(t_ref, c, row, c0))
        return carry

    rows(pass_images)
    for c in range(channels):
        def turn(group, carry, c=c):
            place = pl.ds(pl.multiple_of(group * LANES, LANES), LANES)
            grad_ref[pl.ds(pl.multiple_of((c * (pixels // LANES) + group) * LANES, LANES), LANES)] = jnp.transpose(sum_ref[c, place])
            return carry

        lax.fori_loop(0, pixels // LANES, turn, 0)


def program_body(n_tgt, n_sup, channels, blocks, gathered, counts, *refs):
    refs = list(refs)

    def take(count):
        taken, refs[:count] = refs[:count], []
        return taken

    inputs = take(5 if gathered else 4)
    pred_ref, out_ref = take(2)
    grad_ref, = take(1)
    support = take(1) if gathered else inputs[:1]
    gather_refs = take(counts[0])
    tangent_refs = take(counts[1])

    barrier = pltpu.get_barrier_semaphore()
    for axis, size in (("tgt", n_tgt), ("sup", n_sup)):
        me = lax.axis_index(axis)
        for step in range(1, size):
            pl.semaphore_signal(
                barrier, inc=1, device_id={axis: lax.rem(me + step, size)}, device_id_type=MESH
            )
    pl.semaphore_wait(barrier, n_tgt + n_sup - 2)

    def bring(meanwhile):
        if gathered:
            gather_body(
                n_tgt, channels, blocks, meanwhile, inputs[0], inputs[1], support[0], *gather_refs
            )
        else:
            meanwhile()

    tangent_body(
        bring, n_sup, channels, support[0], *inputs[-3:], pred_ref, grad_ref, *tangent_refs
    )
    sizes, pieces, _ = all_reduce_scratch(grad_ref.shape[0], n_tgt)
    all_reduce_body(sizes, pieces, False, grad_ref, out_ref, *refs)


def local(n_tgt, n_sup, targets, labels, support_slots, block_owner, dual_coeffs):
    blocks, per_block, classes = dual_coeffs.shape
    channels = targets.shape[1]
    pixels = targets.shape[2]
    supports = blocks * per_block
    vmem = pl.BlockSpec(memory_space=pltpu.VMEM)
    smem = pl.BlockSpec(memory_space=pltpu.SMEM)
    flat = pltpu.VMEM((channels * pixels, LANES), jnp.float32)
    gathered = supports == LANES and (pixels * per_block) % (n_tgt * LANES * 8) == 0
    if gathered:
        x = pack_slot(support_slots[0], n_tgt)
        first = (block_owner, x)
        specs = [smem, vmem]
        gather_refs = gather_scratch(x.shape, channels, n_tgt)
    else:
        mine = block_owner == lax.axis_index("tgt")
        slot = jnp.transpose(support_slots[0], (1, 2, 0))
        own = jnp.where(mine[None, None, :, None], slot[:, :, None, :], 0.0)
        own = own.reshape(channels * pixels, supports)
        first = (all_reduce(jnp.pad(own, ((0, 0), (0, LANES - supports))), n_tgt, 0),)
        specs = [vmem]
        gather_refs = []
    field = pltpu.VMEM((SIDE + 2, SIDE + 2, 8, LANES), jnp.float32)
    plain = pltpu.VMEM((SIDE, SIDE, 8, LANES), jnp.float32)
    tangent_refs = [field] * 4 + [plain] * 6 + [
        pltpu.VMEM((channels, SIDE, 8, LANES), jnp.float32),
        pltpu.VMEM((3, SIDE, 8, LANES), jnp.float32),
        pltpu.VMEM((channels, pixels, 1, LANES), jnp.float32),
        pltpu.VMEM((3, pixels, 1, LANES), jnp.float32),
        pltpu.VMEM((2, pixels + 2 * SIDE, LANES), jnp.float32),
        pltpu.VMEM((6, pixels, LANES), jnp.float32),
        pltpu.VMEM((channels, pixels, LANES), jnp.float32),
        pltpu.VMEM((8, classes), jnp.float32),
        pltpu.VMEM((n_sup - 1, 8, classes), jnp.float32),
        pltpu.SemaphoreType.DMA((n_sup - 1,)),
        pltpu.SemaphoreType.DMA((n_sup - 1,)),
    ]
    sum_refs = all_reduce_scratch(channels * pixels, n_tgt)[2]
    predictions, grad = pl.pallas_call(
        functools.partial(
            program_body, n_tgt, n_sup, channels, blocks, gathered,
            (len(gather_refs), len(tangent_refs)),
        ),
        out_shape=(
            jax.ShapeDtypeStruct((8, classes), jnp.float32),
            jax.ShapeDtypeStruct((channels * pixels, LANES), jnp.float32),
        ),
        in_specs=specs + [vmem, smem, vmem],
        out_specs=(vmem, vmem),
        scratch_shapes=[flat] * (1 + gathered) + gather_refs + tangent_refs + sum_refs,
        compiler_params=pltpu.CompilerParams(
            collective_id=1, has_side_effects=True, vmem_limit_bytes=62 << 20
        ),
        name="tangent_kernel",
    )(*first, targets, labels, dual_coeffs)
    grad = grad.reshape(channels, pixels // LANES, LANES, LANES)[:, :, :supports]
    grad = jnp.transpose(grad, (2, 0, 1, 3)).reshape(blocks, per_block, channels, pixels)
    return predictions, grad


def solution(mesh):
    return jax.shard_map(
        functools.partial(local, mesh.shape["tgt"], mesh.shape["sup"]),
        mesh=mesh,
        in_specs=(
            P("tgt", None, None),
            P("tgt"),
            P("tgt", "sup", None, None),
            P(),
            P(None, "sup", None),
        ),
        out_specs=(P("tgt", None), P(None, "sup", None, None)),
        check_vma=False,
    )
```

```python
import functools

import jax
import jax.numpy as jnp
from jax import lax
from jax.experimental import pallas as pl
from jax.experimental.pallas import tpu as pltpu
from jax.sharding import PartitionSpec as P

SIDE = 32
LANES = 128
CHUNK = 8
MESH = pl.DeviceIdType.MESH

weight_variance = 1.6
bias_variance = 0.1
loss_weight = 64.0
q = 2.0 / 3.141592653589793
w9 = weight_variance / 9.0

HALF = (
    0.9999998807907104, 0.16668881475925446, 0.07438822090625763,
    0.05069158226251602, 0.0044584982098147, 0.06837297230958939,
)
MIDDLE = (
    1.0000003576278687, 0.16661593317985535, 0.0763598307967186, 0.03124197944998741,
    0.09119893610477448, -0.11032058298587799, 0.1385442167520523,
)
LAST = (
    0.9999997615814209, 0.16670268774032593, 0.07408007979393005,
    0.0530407689511776, -0.0027404483407735825, 0.07600238919258118,
)


def polynomial(x, coefficients):
    total = jnp.full_like(x, coefficients[-1])
    for value in coefficients[-2::-1]:
        total = total * x + value
    return total


def wide_arcsin(z, complement, r):
    cosine = complement * r
    half = z * lax.rsqrt(2.0 + 2.0 * cosine)
    return (half + half) * polynomial(0.5 - 0.5 * cosine, HALF)


def stage_sizes(devices):
    bits = devices.bit_length() - 1
    low = max((bits - 1) // 2, 0)
    return [size for size in (min(devices, 2), 2 ** low, 2 ** (bits - 1 - low)) if size > 1]


class Stages:
    def __init__(self, sizes):
        self.sizes = sizes
        self.me = lax.axis_index("tgt")
        self.strides, self.digits = [], []
        stride = 1
        for size in sizes:
            self.strides.append(stride)
            self.digits.append(lax.rem(self.me // stride, size))
            stride = stride * size

    def place(self, device):
        total = 0
        for size, stride in zip(self.sizes, self.strides):
            total = total * size + lax.rem(device // stride, size)
        return total

    def peer(self, stage, step):
        digit = lax.rem(self.digits[stage] + step, self.sizes[stage])
        return digit, self.me + (digit - self.digits[stage]) * self.strides[stage]

    def base(self, stage, rows):
        total = 0
        for size, digit in zip(self.sizes[:stage + 1], self.digits):
            rows = rows // size
            total = total + digit * rows
        return total

    def back_copies(self, out_ref, piece, first, rows, stage, send, receive):
        held = rows
        for size in self.sizes[:stage + 1]:
            held = held // size
        place = pl.ds(pl.multiple_of(first + self.base(stage, rows), 8), held)
        before = sum(size - 1 for size in self.sizes[:stage])
        copies = []
        for step in range(1, self.sizes[stage]):
            copies.append(pltpu.make_async_remote_copy(
                src_ref=out_ref.at[place],
                dst_ref=out_ref.at[place],
                send_sem=send.at[piece, before + step - 1],
                recv_sem=receive.at[piece, before + step - 1],
                device_id={"tgt": self.peer(stage, step)[1]},
                device_id_type=MESH,
            ))
        return copies


def start_all(copies):
    for copy in copies:
        copy.start()
    return copies


def all_reduce_body(sizes, pieces, greet, produce, x_ref, out_ref, *scratch):
    stages = len(sizes)
    received = scratch[:stages]
    partial = scratch[stages:2 * stages - 1]
    send_sem, recv_sem, send_back, recv_back = scratch[2 * stages - 1:]
    where = Stages(sizes)
    if greet:
        barrier = pltpu.get_barrier_semaphore()
        for stage, size in enumerate(sizes):
            for step in range(1, size):
                pl.semaphore_signal(
                    barrier, inc=1, device_id={"tgt": where.peer(stage, step)[1]},
                    device_id_type=MESH,
                )
        pl.semaphore_wait(barrier, sum(size - 1 for size in sizes))
    rows = x_ref.shape[0] // pieces
    held = [rows]
    for size in sizes:
        held.append(held[-1] // size)

    def source(stage, piece):
        if stage == 0:
            return x_ref.at[pl.ds(piece * rows, rows)]
        return partial[stage - 1].at[piece]

    def send(stage, piece):
        size = sizes[stage]
        before = sum(other - 1 for other in sizes[:stage])
        copies = []
        for step in range(1, size):
            digit, device = where.peer(stage, step)
            part = pl.ds(pl.multiple_of(digit * held[stage + 1], 8), held[stage + 1])
            copies.append(pltpu.make_async_remote_copy(
                src_ref=source(stage, piece).at[part],
                dst_ref=received[stage].at[piece, step - 1],
                send_sem=send_sem.at[piece, before + step - 1],
                recv_sem=recv_sem.at[piece, before + step - 1],
                device_id={"tgt": device},
                device_id_type=MESH,
            ))
        return start_all(copies)

    def add(stage, piece, copies):
        part = pl.ds(
            pl.multiple_of(where.digits[stage] * held[stage + 1], 8), held[stage + 1]
        )
        total = source(stage, piece)[part]
        for copy in copies:
            copy.wait()
        for slot in range(sizes[stage] - 1):
            total = total + received[stage][piece, slot]
        if stage + 1 < stages:
            partial[stage][piece] = total
        else:
            place = pl.multiple_of(piece * rows + where.base(stage, rows), 8)
            out_ref[pl.ds(place, held[stage + 1])] = total

    def back(step, piece):
        return start_all(where.back_copies(
            out_ref, piece, piece * rows, rows, stages - 1 - step, send_back, recv_back
        ))

    pending = []
    for piece in range(pieces):
        produce(piece)
        pending.append(send(0, piece))
    for tick in range(pieces + 2 * stages - 1):
        for piece in range(pieces):
            level = tick - piece
            if level < 0 or level >= 2 * stages:
                continue
            if level < stages:
                add(level, piece, pending[piece])
            else:
                for copy in pending[piece]:
                    copy.wait()
            if level + 1 < stages:
                pending[piece] = send(level + 1, piece)
            elif level + 1 < 2 * stages:
                pending[piece] = back(level + 1 - stages, piece)


def all_reduce_scratch(rows, devices):
    sizes = stage_sizes(devices)
    pieces = max(k for k in (1, 2, 3) if rows % (k * devices * 8) == 0)
    rows = rows // pieces
    received, partial = [], []
    for size in sizes:
        rows = rows // size
        received.append(pltpu.VMEM((pieces, size - 1, rows, LANES), jnp.float32))
        partial.append(pltpu.VMEM((pieces, rows, LANES), jnp.float32))
    copies = sum(size - 1 for size in sizes)
    semaphores = [pltpu.SemaphoreType.DMA((pieces, copies))] * 4
    return sizes, pieces, received + partial[:-1] + semaphores


def all_reduce(x, devices, collective_id):
    sizes, pieces, scratch = all_reduce_scratch(x.shape[0], devices)
    return pl.pallas_call(
        functools.partial(all_reduce_body, sizes, pieces, True, lambda piece: None),
        out_shape=jax.ShapeDtypeStruct(x.shape, x.dtype),
        in_specs=[pl.BlockSpec(memory_space=pltpu.VMEM)],
        out_specs=pl.BlockSpec(memory_space=pltpu.VMEM),
        scratch_shapes=scratch,
        compiler_params=pltpu.CompilerParams(
            collective_id=collective_id, has_side_effects=True, vmem_limit_bytes=24 << 20
        ),
        name="sum_over_targets",
    )(x)


def gather_body(devices, channels, blocks, meanwhile, owner_ref, x_ref, out_ref, *scratch):
    slots = scratch[:channels]
    send_sem, recv_sem, send_back, recv_back = scratch[channels:]
    sizes = stage_sizes(devices)
    stages = len(sizes)
    where = Stages(sizes)
    me = where.me
    packed = x_ref.shape[1] // channels
    copies = []
    for c in range(channels):
        part = pl.ds(c * packed, packed)
        copies.append([])
        for step in range(1, devices):
            device = lax.rem(me + step, devices)
            copies[c].append(pltpu.make_async_remote_copy(
                src_ref=x_ref.at[where.place(device), part],
                dst_ref=slots[c].at[me],
                send_sem=send_sem.at[c, step - 1],
                recv_sem=recv_sem.at[c, step - 1],
                device_id={"tgt": device},
                device_id_type=MESH,
            ))
        start_all(copies[c])
    for c in range(channels):
        slots[c][me] = x_ref[where.place(me), pl.ds(c * packed, packed)]
    meanwhile()
    rows = out_ref.shape[0] // channels
    chunk = rows // devices
    groups = chunk // packed
    width = LANES // groups
    block = lax.broadcasted_iota(jnp.int32, (packed, LANES), 1) // width
    base = where.base(stages - 1, rows)
    pending = []
    for c in range(channels):
        for copy in copies[c]:
            copy.wait()
        parts = [slots[c][owner_ref[b]] for b in range(blocks)]
        for k in range(groups):
            total = jnp.zeros((packed, LANES), jnp.float32)
            for b in range(blocks):
                shift = (width * (b - k)) % LANES
                moved = pltpu.roll(parts[b], shift, 1) if shift else parts[b]
                total = jnp.where(block == b, moved, total)
            out_ref[pl.ds(pl.multiple_of(c * rows + base + k * packed, 8), packed)] = total
        pending.append(start_all(where.back_copies(
            out_ref, c, c * rows, rows, stages - 1, send_back, recv_back
        )))
    for tick in range(channels + stages - 1):
        for c in range(channels):
            level = tick - c
            if level < 0 or level >= stages:
                continue
            for copy in pending[c]:
                copy.wait()
            if level + 1 < stages:
                pending[c] = start_all(where.back_copies(
                    out_ref, c, c * rows, rows, stages - 2 - level, send_back, recv_back
                ))


def pack_slot(slot, devices):
    per_block, channels, pixels = slot.shape
    groups = LANES // per_block
    packed = pixels // devices // groups
    x = slot.reshape(per_block, channels, devices, groups, packed)
    return jnp.transpose(x, (2, 1, 4, 3, 0)).reshape(devices, channels * packed, LANES)


def gather_scratch(packed_shape, channels, devices):
    _, rows, _ = packed_shape
    copies = sum(size - 1 for size in stage_sizes(devices))
    return [pltpu.VMEM((devices, rows // channels, LANES), jnp.float32)] * channels + [
        pltpu.SemaphoreType.DMA((channels, devices - 1)),
        pltpu.SemaphoreType.DMA((channels, devices - 1)),
        pltpu.SemaphoreType.DMA((channels, copies)),
        pltpu.SemaphoreType.DMA((channels, copies)),
    ]


def tangent_body(
    bring, n_sup, channels, s_ref, raw_ref, label_ref, dual_ref, pred_ref, grad_ref,
    f1, f2, f3, f4, z1_ref, r1_ref, z2_ref, r2_ref, th2_ref, n3_ref, t_ref, u_ref, sb_ref,
    vb_ref, sf_ref, nb_ref, sum_ref, part_ref, arrived, send_sem, recv_sem,
):
    pixels = SIDE * SIDE
    me = lax.axis_index("sup")

    def prepare():
        lane = lax.broadcasted_iota(jnp.int32, (8, LANES), 1)
        t_ref[...] = jnp.zeros(t_ref.shape, jnp.float32)
        for c in range(channels):
            image = raw_ref[:, c, :]
            for row in range(SIDE):
                t_ref[c, row, :, :SIDE] = image[:, row * SIDE:(row + 1) * SIDE]

        def lane_box(x):
            none = jnp.zeros((1, 8, LANES), jnp.float32)
            total = x + jnp.concatenate([none, x[:-1]]) + jnp.concatenate([x[1:], none])
            left = jnp.where(lane == 0, 0.0, pltpu.roll(total, 1, 2))
            right = jnp.where(lane == SIDE - 1, 0.0, pltpu.roll(total, LANES - 1, 2))
            return total + left + right

        power = t_ref[0] * t_ref[0]
        for c in range(1, channels):
            power = power + t_ref[c] * t_ref[c]
        n_t = (w9 / channels) * lane_box(power) + bias_variance
        for layer in range(3):
            b_t = 1.0 + 2.0 * n_t
            u_ref[layer] = lax.rsqrt(b_t)
            if layer < 2:
                z_t = 2.0 * n_t / b_t
                if layer == 0:
                    rest = 1.0 - z_t * z_t
                    angle_t = wide_arcsin(z_t, rest, lax.rsqrt(rest))
                else:
                    angle_t = z_t * polynomial(z_t * z_t, MIDDLE)
                angle_t = jnp.where(lane < SIDE, angle_t, 0.0)
                n_t = (w9 * q) * lane_box(angle_t) + bias_variance

        for field in (f1, f2, f3, f4):
            for row in (0, SIDE + 1):
                field[row] = jnp.zeros(field.shape[1:], jnp.float32)

            def border(row, carry, field=field):
                for column in (0, SIDE + 1):
                    field[row, column] = jnp.zeros(field.shape[2:], jnp.float32)
                return carry

            lax.fori_loop(1, SIDE + 1, border, 0)

    bring(prepare)

    zero_row = jnp.zeros((SIDE, LANES), jnp.float32)
    for slot in range(2):
        sf_ref[slot, pl.ds(0, SIDE)] = zero_row
        sf_ref[slot, pl.ds(SIDE + pixels, SIDE)] = zero_row
    column = lax.broadcasted_iota(jnp.int32, (SIDE, LANES), 0)

    def line(row):
        return pl.ds(pl.multiple_of(row * SIDE, SIDE), SIDE)

    def flat_box(slot, row):
        x = (
            sf_ref[slot, line(row)] + sf_ref[slot, line(row + 1)] + sf_ref[slot, line(row + 2)]
        )
        left = jnp.where(column == 0, 0.0, pltpu.roll(x, 1, 0))
        right = jnp.where(column == SIDE - 1, 0.0, pltpu.roll(x, SIDE - 1, 0))
        return x + left + right

    def squares(row, carry):
        total = jnp.zeros((SIDE, LANES), jnp.float32)
        for c in range(channels):
            image = s_ref[pl.ds(pl.multiple_of(c * pixels + row * SIDE, SIDE), SIDE)]
            total = total + image * image
            for j in range(SIDE):
                sb_ref[c, row * SIDE + j] = image[j:j + 1]
        sf_ref[0, line(row + 1)] = total
        return carry

    lax.fori_loop(0, SIDE, squares, 0)

    def own_layer(layer):
        source, target = layer % 2, (layer + 1) % 2
        scale = w9 / channels if layer == 0 else w9 * q

        def body(row, carry):
            n = scale * flat_box(source, row) + bias_variance
            b = 1.0 + 2.0 * n
            v = lax.rsqrt(b)
            nb_ref[layer, line(row)] = n
            for j in range(SIDE):
                vb_ref[layer, row * SIDE + j] = v[j:j + 1]
            if layer < 2:
                z = 2.0 * n / b
                if layer == 0:
                    complement = 1.0 - z * z
                    angle = wide_arcsin(z, complement, lax.rsqrt(complement))
                else:
                    angle = z * polynomial(z * z, MIDDLE)
                sf_ref[target, line(row + 1)] = angle
            return carry

        lax.fori_loop(0, SIDE, body, 0)

    for layer in range(3):
        own_layer(layer)

    coeffs = dual_ref[...].reshape(-1, dual_ref.shape[2])
    if coeffs.shape[0] < LANES:
        coeffs = jnp.pad(coeffs, ((0, LANES - coeffs.shape[0]), (0, 0)))

    def rows(function, init=0):
        def four(step, carry):
            return function(step * 4 + 2, function(step * 4, carry))

        return lax.fori_loop(0, SIDE // 4, four, init)

    def spread(ref, k, row, c0):
        values = ref[k, row]
        return jnp.stack(
            [jnp.broadcast_to(values[:, c0 + j:c0 + j + 1], (8, LANES)) for j in range(CHUNK)]
        )

    def across(ref, k, row, c0):
        values = ref[k, pl.ds(row * SIDE + c0, CHUNK)]
        return jnp.broadcast_to(values, (CHUNK, 8, LANES))

    def box(ref, row, c0):
        lines = [ref[row + k, pl.ds(c0, CHUNK + 2)] for k in range(4)]
        middle = lines[1] + lines[2]
        sums = [lines[0] + middle, middle + lines[3]]
        return [x[:-2] + x[1:-1] + x[2:] for x in sums]

    def put(ref, row, c0, value):
        ref[row + 1, pl.ds(c0 + 1, CHUNK)] = value

    def keep(ref, row, c0, value):
        ref[row, pl.ds(c0, CHUNK)] = value

    def kept(ref, row, c0):
        return ref[row, pl.ds(c0, CHUNK)]

    starts = range(0, SIDE, CHUNK)

    def pass_cross(first, carry):
        for row in (first, first + 1):
            for c0 in starts:
                total = spread(t_ref, 0, row, c0) * across(sb_ref, 0, row, c0)
                for c in range(1, channels):
                    total = total + spread(t_ref, c, row, c0) * across(sb_ref, c, row, c0)
                put(f1, row, c0, total)
        return carry

    def pass_first(first, carry):
        for c0 in starts:
            for row, value in zip((first, first + 1), box(f1, first, c0)):
                uv = spread(u_ref, 0, row, c0) * across(vb_ref, 0, row, c0)
                z = uv * ((2.0 * w9 / channels) * value + 2.0 * bias_variance)
                complement = 1.0 - z * z
                r = lax.rsqrt(complement)
                keep(z1_ref, row, c0, z)
                keep(r1_ref, row, c0, r)
                put(f2, row, c0, wide_arcsin(z, complement, r))
                put(f3, row, c0, z * r)
        return carry

    def pass_second(first, carry):
        for c0 in starts:
            pairs = zip((first, first + 1), box(f2, first, c0), box(f3, first, c0))
            for row, angles, tangents in pairs:
                uv = spread(u_ref, 1, row, c0) * across(vb_ref, 1, row, c0)
                z = uv * ((2.0 * w9 * q) * angles + 2.0 * bias_variance)
                tangent = z + uv * ((2.0 * w9 * q) * tangents)
                square = z * z
                r = lax.rsqrt(1.0 - square)
                keep(z2_ref, row, c0, z)
                keep(r2_ref, row, c0, r)
                keep(th2_ref, row, c0, tangent)
                put(f1, row, c0, z * polynomial(square, MIDDLE))
                put(f4, row, c0, tangent * r)
        return carry

    def pass_third(first, carry):
        for c0 in starts:
            pairs = zip((first, first + 1), box(f1, first, c0), box(f4, first, c0))
            for row, angles, tangents in pairs:
                uv = spread(u_ref, 2, row, c0) * across(vb_ref, 2, row, c0)
                z = uv * ((2.0 * w9 * q) * angles + 2.0 * bias_variance)
                tangent = z + uv * ((2.0 * w9 * q) * tangents)
                square = z * z
                r = lax.rsqrt(1.0 - square)
                carry = carry + jnp.sum(z * polynomial(square, LAST) + tangent * r, axis=0)
                slope = (2.0 * q * w9) * (uv * r)
                bent = tangent * (r * r)
                put(f3, row, c0, slope)
                put(f2, row, c0, slope * (2.0 + z * bent))
                keep(n3_ref, row, c0, r * (z + bent))
        return carry

    rows(pass_cross)
    rows(pass_first)
    rows(pass_second)
    mean = rows(pass_third, jnp.zeros((8, LANES), jnp.float32))
    kernel = (weight_variance * q / pixels) * mean + bias_variance

    part_ref[...] = jnp.dot(
        kernel, coeffs, precision=lax.Precision.HIGHEST,
        preferred_element_type=jnp.float32,
    )
    copies = []
    for step in range(1, n_sup):
        copy = pltpu.make_async_remote_copy(
            src_ref=part_ref,
            dst_ref=arrived.at[step - 1],
            send_sem=send_sem.at[step - 1],
            recv_sem=recv_sem.at[step - 1],
            device_id={"sup": lax.rem(me + step, n_sup)},
            device_id_type=MESH,
        )
        copy.start()
        copies.append(copy)
    for copy in copies:
        copy.wait()
    predictions = part_ref[...]
    for step in range(n_sup - 1):
        predictions = predictions + arrived[step]
    pred_ref[...] = predictions
    target = lax.broadcasted_iota(jnp.int32, predictions.shape, 0)
    label = jnp.zeros(predictions.shape, jnp.int32)
    for k in range(8):
        label = jnp.where(target == k, label_ref[k], label)
    onehot = (label == lax.broadcasted_iota(jnp.int32, predictions.shape, 1)).astype(jnp.float32)
    error = loss_weight * (predictions - onehot)
    weights = lax.dot_general(
        error, coeffs, (((1,), (1,)), ((), ())), precision=lax.Precision.HIGHEST,
        preferred_element_type=jnp.float32,
    )
    kappa = (weight_variance / pixels) * weights

    sublane = lax.broadcasted_iota(jnp.int32, (8, LANES), 0)
    odd = [lax.rem(sublane // step, 2) == 1 for step in (1, 2, 4)]

    def total_rows(value):
        items = [value[j] for j in range(CHUNK)]
        for step, mask in zip((1, 2, 4), odd):
            items = [
                jnp.where(mask, second, first)
                + pltpu.roll(jnp.where(mask, first, second), step, 0)
                for first, second in zip(items[::2], items[1::2])
            ]
        return items[0]

    def pass_back_second(first, carry):
        for c0 in starts:
            pairs = zip((first, first + 1), box(f2, first, c0), box(f3, first, c0))
            for row, up, mean_up in pairs:
                uv = spread(u_ref, 1, row, c0) * across(vb_ref, 1, row, c0)
                z = kept(z2_ref, row, c0)
                r = kept(r2_ref, row, c0)
                up = kappa * up
                mean_up = kappa * mean_up
                bent = mean_up * kept(th2_ref, row, c0) * (r * r)
                slope = (2.0 * q * w9) * (uv * r)
                put(f4, row, c0, mean_up * slope)
                put(f1, row, c0, slope * (up + mean_up + bent * z))
                place = pl.ds(pl.multiple_of(row * SIDE + c0, CHUNK), CHUNK)
                nb_ref[4, place] = total_rows(r * (up * z + bent))
                nb_ref[5, place] = total_rows(kappa * kept(n3_ref, row, c0))
        return carry

    def pass_back_first(first, carry):
        for c0 in starts:
            pairs = zip((first, first + 1), box(f1, first, c0), box(f4, first, c0))
            for row, up, mean_up in pairs:
                uv = spread(u_ref, 0, row, c0) * across(vb_ref, 0, row, c0)
                r = kept(r1_ref, row, c0)
                joined = r * (up + (r * r) * mean_up)
                put(f2, row, c0, (2.0 * q * w9 / channels) * (uv * joined))
                place = pl.ds(pl.multiple_of(row * SIDE + c0, CHUNK), CHUNK)
                nb_ref[3, place] = total_rows(kept(z1_ref, row, c0) * joined)
        return carry

    rows(pass_back_second)
    rows(pass_back_first)

    def own_back(layer):
        source, target = (layer + 1) % 2, layer % 2

        def body(row, carry):
            n = nb_ref[layer, line(row)]
            b = 1.0 + 2.0 * n
            value = nb_ref[3 + layer, line(row)] * (-q / b)
            if layer < 2:
                value = value + (2.0 * w9 * q) * flat_box(source, row) * (
                    lax.rsqrt(1.0 + 4.0 * n) / b
                )
            sf_ref[target, line(row + 1)] = value
            return carry

        lax.fori_loop(0, SIDE, body, 0)

    for layer in (2, 1, 0):
        own_back(layer)

    def produce(c):
        def pass_image(first, carry):
            for row in (first, first + 1):
                own = (2.0 * w9 / channels) * flat_box(0, row)
                image = s_ref[pl.ds(pl.multiple_of(c * pixels + row * SIDE, SIDE), SIDE)]
                sum_ref[c, line(row)] = own * image
            for c0 in starts:
                if c == 0:
                    values = box(f2, first, c0)
                else:
                    values = [kept(z1_ref, row, c0) for row in (first, first + 1)]
                for row, value in zip((first, first + 1), values):
                    if c == 0:
                        keep(z1_ref, row, c0, value)
                    place = pl.ds(pl.multiple_of(row * SIDE + c0, CHUNK), CHUNK)
                    sum_ref[c, place] += total_rows(value * spread(t_ref, c, row, c0))
            return carry

        rows(pass_image)

        def turn(group, carry):
            place = pl.ds(pl.multiple_of(group * LANES, LANES), LANES)
            first = pl.multiple_of((c * (pixels // LANES) + group) * LANES, LANES)
            grad_ref[pl.ds(first, LANES)] = jnp.transpose(sum_ref[c, place])
            return carry

        lax.fori_loop(0, pixels // LANES, turn, 0)

    return produce


def program_body(n_tgt, n_sup, channels, blocks, gathered, counts, *refs):
    refs = list(refs)

    def take(count):
        taken, refs[:count] = refs[:count], []
        return taken

    inputs = take(5 if gathered else 4)
    pred_ref, out_ref = take(2)
    grad_ref, = take(1)
    support = take(1) if gathered else inputs[:1]
    gather_refs = take(counts[0])
    tangent_refs = take(counts[1])

    barrier = pltpu.get_barrier_semaphore()
    for axis, size in (("tgt", n_tgt), ("sup", n_sup)):
        me = lax.axis_index(axis)
        for step in range(1, size):
            pl.semaphore_signal(
                barrier, inc=1, device_id={axis: lax.rem(me + step, size)}, device_id_type=MESH
            )
    pl.semaphore_wait(barrier, n_tgt + n_sup - 2)

    def bring(meanwhile):
        if gathered:
            gather_body(
                n_tgt, channels, blocks, meanwhile, inputs[0], inputs[1], support[0], *gather_refs
            )
        else:
            meanwhile()

    channel = tangent_body(
        bring, n_sup, channels, support[0], *inputs[-3:], pred_ref, grad_ref, *tangent_refs
    )
    sizes, pieces, _ = all_reduce_scratch(grad_ref.shape[0], n_tgt)

    def produce(piece):
        if pieces == channels:
            channel(piece)
        elif piece == 0:
            for c in range(channels):
                channel(c)

    all_reduce_body(sizes, pieces, False, produce, grad_ref, out_ref, *refs)


def local(n_tgt, n_sup, targets, labels, support_slots, block_owner, dual_coeffs):
    blocks, per_block, classes = dual_coeffs.shape
    channels = targets.shape[1]
    pixels = targets.shape[2]
    supports = blocks * per_block
    vmem = pl.BlockSpec(memory_space=pltpu.VMEM)
    smem = pl.BlockSpec(memory_space=pltpu.SMEM)
    flat = pltpu.VMEM((channels * pixels, LANES), jnp.float32)
    gathered = supports == LANES and (pixels * per_block) % (n_tgt * LANES * 8) == 0
    if gathered:
        x = pack_slot(support_slots[0], n_tgt)
        first = (block_owner, x)
        specs = [smem, vmem]
        gather_refs = gather_scratch(x.shape, channels, n_tgt)
    else:
        mine = block_owner == lax.axis_index("tgt")
        slot = jnp.transpose(support_slots[0], (1, 2, 0))
        own = jnp.where(mine[None, None, :, None], slot[:, :, None, :], 0.0)
        own = own.reshape(channels * pixels, supports)
        first = (all_reduce(jnp.pad(own, ((0, 0), (0, LANES - supports))), n_tgt, 0),)
        specs = [vmem]
        gather_refs = []
    field = pltpu.VMEM((SIDE + 2, SIDE + 2, 8, LANES), jnp.float32)
    plain = pltpu.VMEM((SIDE, SIDE, 8, LANES), jnp.float32)
    tangent_refs = [field] * 4 + [plain] * 6 + [
        pltpu.VMEM((channels, SIDE, 8, LANES), jnp.float32),
        pltpu.VMEM((3, SIDE, 8, LANES), jnp.float32),
        pltpu.VMEM((channels, pixels, 1, LANES), jnp.float32),
        pltpu.VMEM((3, pixels, 1, LANES), jnp.float32),
        pltpu.VMEM((2, pixels + 2 * SIDE, LANES), jnp.float32),
        pltpu.VMEM((6, pixels, LANES), jnp.float32),
        pltpu.VMEM((channels, pixels, LANES), jnp.float32),
        pltpu.VMEM((8, classes), jnp.float32),
        pltpu.VMEM((n_sup - 1, 8, classes), jnp.float32),
        pltpu.SemaphoreType.DMA((n_sup - 1,)),
        pltpu.SemaphoreType.DMA((n_sup - 1,)),
    ]
    sum_refs = all_reduce_scratch(channels * pixels, n_tgt)[2]
    predictions, grad = pl.pallas_call(
        functools.partial(
            program_body, n_tgt, n_sup, channels, blocks, gathered,
            (len(gather_refs), len(tangent_refs)),
        ),
        out_shape=(
            jax.ShapeDtypeStruct((8, classes), jnp.float32),
            jax.ShapeDtypeStruct((channels * pixels, LANES), jnp.float32),
        ),
        in_specs=specs + [vmem, smem, vmem],
        out_specs=(vmem, vmem),
        scratch_shapes=[flat] * (1 + gathered) + gather_refs + tangent_refs + sum_refs,
        compiler_params=pltpu.CompilerParams(
            collective_id=1, has_side_effects=True, vmem_limit_bytes=62 << 20
        ),
        name="tangent_kernel",
    )(*first, targets, labels, dual_coeffs)
    grad = grad.reshape(channels, pixels // LANES, LANES, LANES)[:, :, :supports]
    grad = jnp.transpose(grad, (2, 0, 1, 3)).reshape(blocks, per_block, channels, pixels)
    return predictions, grad


def solution(mesh):
    return jax.shard_map(
        functools.partial(local, mesh.shape["tgt"], mesh.shape["sup"]),
        mesh=mesh,
        in_specs=(
            P("tgt", None, None),
            P("tgt"),
            P("tgt", "sup", None, None),
            P(),
            P(None, "sup", None),
        ),
        out_specs=(P("tgt", None), P(None, "sup", None, None)),
        check_vma=False,
    )
```
